32 devices in a mesh: ctx: 16 (over z, y, core), mp: 2 (over x).
Axes of the slice: x: 2, y: 2, z: 4, core: 2. Of those that a mesh axis runs over, the one named last changes fastest.
Arguments:
- stream: bfloat16 [4, 65536, 1024], P(None, 'ctx', 'mp'), may hold values from -40 to 40
- gain_mix: bfloat16 [1024], P('mp'), may hold values from 0.25 to 1.75
- proj_in: bfloat16 [8, 128, 384], P('mp'), may hold values from -0.5 to 0.5
- short_taps: float32 [3, 8, 384], P(None, 'mp'), may hold values from -3 to 3
- fwd_inner: bfloat16 [256, 256], replicated, may hold values from -0.375 to 0.375
- twid_inner: float32 [256, 256], P('ctx'), may hold values from -1.5 to 1.5
- fwd_outer: bfloat16 [256, 256], replicated, may hold values from -0.375 to 0.375
- kernel: bfloat16 [256, 256, 1024], P(None, 'ctx', 'mp'), may hold values from -4 to 4
- inv_outer: bfloat16 [256, 256], replicated, may hold values from -0.375 to 0.375
- backward_twiddle: float32 [256, 256], P(None, 'ctx'), may hold values from -1.5 to 1.5
- inv_inner: bfloat16 [256, 256], replicated, may hold values from -0.375 to 0.375
- proj_out: bfloat16 [8, 128, 128], P('mp'), may hold values from -0.5 to 0.5
- gain_mlp: bfloat16 [1024], P('mp'), may hold values from 0.25 to 1.75
- up_blocks: bfloat16 [8, 128, 512], P('mp'), may hold values from -0.5 to 0.5
- down_blocks: bfloat16 [8, 512, 128], P('mp'), may hold values from -0.25 to 0.25
Outputs:
- stream_out: bfloat16 [4, 65536, 1024], P(None, 'ctx', 'mp')
The draws below stay inside these ranges and needn't reach their ends.
All inputs are finite; a program needn't handle non-finite values.
Results may differ from the reference program's by a relative error of at most 0.0085.
Values may be sent and summed in bfloat16 or wider, within the bound.
No kernel may reach another device: no remote copies, remote signals or barrier semaphores. Data moves between devices by JAX's collectives and lax.ppermute only.
A program may use at most 320 MiB of HBM per device.

```python
import jax
import jax.numpy as jnp
from jax import lax

D = 1024
FF = 4096
NB = 8
ROOT = 256
SEQS = 4
SEQ_LEN = 65536
CB = 128
HB = 512


def draw_stream(key, part):
    key_base, key_col, key_row = jax.random.split(key, 3)
    span = jnp.arange(D, dtype=jnp.float32) / D
    column_scale = jnp.exp(jnp.log(3.0) * span + jax.random.uniform(key_col, (D,), jnp.float32, 0.0, jnp.log(3.3))) / 3.0
    row_scale = jnp.exp(jax.random.uniform(key_row, (SEQS, SEQ_LEN, 1), jnp.float32, jnp.log(0.3), jnp.log(3.0)))
    base = jnp.clip(jax.random.normal(key_base, (SEQS, SEQ_LEN, D), jnp.float32), -4.0, 4.0)
    return (base * row_scale * column_scale).astype(jnp.bfloat16)


def levels(key, extent, cuts, smallest, top_value):
    def one(position, blocks):
        draws = jax.random.uniform(jax.random.fold_in(jax.random.fold_in(key, 6), position), (blocks,), jnp.float32, smallest / len(cuts), top_value / len(cuts))
        return jnp.repeat(jnp.exp(draws), extent[position] // blocks).reshape((-1,) + (1,) * (len(extent) - position - 1))

    gain = one(*cuts[0])
    for cut in cuts[1:]:
        gain = gain * one(*cut)
    return gain


def scatter_about(stream_key, extent, scale, most, shards=(), kind=jnp.bfloat16):
    values = jax.random.normal(stream_key, extent, jnp.float32) * scale
    if len(shards) > 0:
        values = levels(stream_key, extent, shards, -0.22, 0.18) * values
    return jnp.clip(values, min=-most, max=most).astype(kind)


def setup_inputs(seed: int = 0) -> dict:
    key_list = jax.random.split(jax.random.key(seed), 16)
    stream = draw_stream(jax.random.fold_in(key_list[15], 71), 0)
    gain_mix = jnp.clip(1.0 + 0.15 * jax.random.normal(key_list[1], (D,), jnp.float32), 0.25, 1.75).astype(jnp.bfloat16)
    proj_in = scatter_about(key_list[2], (NB, CB, 3 * CB), CB ** -0.5, 0.5, ((0, 2),))
    short_taps = scatter_about(key_list[3], (3, NB, 3 * CB), 0.5, 3.0, ((1, 2),), jnp.float32)
    fwd_inner = scatter_about(key_list[4], (ROOT, ROOT), ROOT ** -0.5, 0.375)
    twid_inner = jnp.clip(jax.random.uniform(key_list[5], (ROOT, ROOT), jnp.float32, -1.5, 1.5) * levels(key_list[5], (ROOT, ROOT), ((0, 16),), -0.4, 0.0), -1.5, 1.5)
    fwd_outer = scatter_about(key_list[6], (ROOT, ROOT), ROOT ** -0.5, 0.375)
    kernel = scatter_about(key_list[7], (ROOT, ROOT, D), 1.0, 4.0, ((1, 16), (2, 2)))
    inv_outer = scatter_about(key_list[8], (ROOT, ROOT), ROOT ** -0.5, 0.375)
    backward_twiddle = jnp.clip(jax.random.uniform(key_list[9], (ROOT, ROOT), jnp.float32, -1.5, 1.5) * levels(key_list[9], (ROOT, ROOT), ((1, 16),), -0.4, 0.0), -1.5, 1.5)
    inv_inner = scatter_about(key_list[10], (ROOT, ROOT), ROOT ** -0.5, 0.375)
    proj_out = scatter_about(key_list[11], (NB, CB, CB), CB ** -0.5, 0.5, ((0, 2),))
    gain_mlp = jnp.clip(1.0 + 0.15 * jax.random.normal(key_list[12], (D,), jnp.float32), 0.25, 1.75).astype(jnp.bfloat16)
    up_blocks = scatter_about(key_list[13], (NB, CB, HB), CB ** -0.5, 0.5, ((0, 2),))
    down_blocks = scatter_about(key_list[14], (NB, HB, CB), HB ** -0.5, 0.25, ((0, 2),))
    return dict(stream=stream, gain_mix=gain_mix, proj_in=proj_in, short_taps=short_taps, fwd_inner=fwd_inner, twid_inner=twid_inner, fwd_outer=fwd_outer, kernel=kernel, inv_outer=inv_outer, backward_twiddle=backward_twiddle, inv_inner=inv_inner, proj_out=proj_out, gain_mlp=gain_mlp, up_blocks=up_blocks, down_blocks=down_blocks)


epsilon = 1e-05

def cast_bfloat16(value):
    return lax.optimization_barrier(value.astype(jnp.bfloat16))

def reference(stream, gain_mix, proj_in, short_taps, fwd_inner, twid_inner, fwd_outer, kernel, inv_outer, backward_twiddle, inv_inner, proj_out, gain_mlp, up_blocks, down_blocks):
    block_width = D // NB
    sub_width = block_width // NB
    hid_block = FF // NB
    hid_sub = hid_block // NB
    upper_half = lax.Precision.HIGHEST
    kernel_blocks = jnp.moveaxis(kernel.reshape(ROOT, ROOT, NB, block_width), 2, 0)
    tap_blocks = jnp.moveaxis(short_taps, 1, 0)
    fwd_in = fwd_inner.astype(jnp.float32)
    forward_result = fwd_outer.astype(jnp.float32)
    inverse_result = inv_outer.astype(jnp.float32)
    inv_in = inv_inner.astype(jnp.float32)

    def mixer_block(portion):
        block_in, weight_in, tap_part, kernel_piece = portion
        projected = cast_bfloat16(jnp.dot(block_in, weight_in, preferred_element_type=jnp.float32)).astype(jnp.float32)
        back_one = jnp.concatenate([jnp.zeros((1, 3 * block_width), jnp.float32), projected[:-1]], 0)
        back_two = jnp.concatenate([jnp.zeros((2, 3 * block_width), jnp.float32), projected[:-2]], 0)
        mixed_all = tap_part[0] * projected + tap_part[1] * back_one + tap_part[2] * back_two
        query_part = mixed_all[:, :block_width].astype(jnp.bfloat16)
        source = (mixed_all[:, block_width:2 * block_width] * mixed_all[:, 2 * block_width:]).astype(jnp.bfloat16)
        lattice = source.astype(jnp.float32).reshape(ROOT, ROOT, block_width)
        opening_segment = cast_bfloat16(jnp.einsum('abc,bf->afc', lattice, fwd_in, precision=upper_half) * twid_inner[:, :, None]).astype(jnp.float32)
        middle_segment = cast_bfloat16(jnp.einsum('hwd,hl->lwd', opening_segment, forward_result, precision=upper_half) * kernel_piece.astype(jnp.float32)).astype(jnp.float32)
        closing_segment = cast_bfloat16(jnp.einsum('njk,nz->zjk', middle_segment, inverse_result, precision=upper_half) * backward_twiddle[:, :, None]).astype(jnp.float32)
        convolved = jnp.einsum('hfc,fe->hec', closing_segment, inv_in, precision=upper_half).reshape(SEQ_LEN, block_width)
        return (query_part.astype(jnp.float32) * convolved).astype(jnp.bfloat16)

    def mlp_rows(row_block):
        row_count = row_block.shape[0]
        row_float = row_block.astype(jnp.float32)
        sumsq = lax.optimization_barrier(jnp.sum(row_float * row_float, axis=1, keepdims=True))
        normed_mlp = (row_float * lax.rsqrt(sumsq / D + epsilon) * gain_mlp.astype(jnp.float32)).astype(jnp.bfloat16)
        upper_part = jnp.einsum('lic,ich->lih', normed_mlp.reshape(row_count, NB, block_width).astype(jnp.float32), up_blocks.astype(jnp.float32), precision=upper_half)
        active = jax.nn.gelu(upper_part).astype(jnp.bfloat16)
        permuted = jnp.transpose(active.reshape(row_count, NB, NB, hid_sub), (0, 2, 1, 3)).reshape(row_count, NB, hid_block)
        lower_part = jnp.einsum('ljk,jkd->ljd', permuted.astype(jnp.float32), down_blocks.astype(jnp.float32), precision=upper_half)
        return (row_float + lower_part.reshape(row_count, D)).astype(jnp.bfloat16)

    def one_sequence(sequence):
        seq_float = sequence.astype(jnp.float32)
        sumsq = lax.optimization_barrier(jnp.sum(seq_float * seq_float, axis=1, keepdims=True))
        normed = (seq_float * lax.rsqrt(sumsq / D + epsilon) * gain_mix.astype(jnp.float32)).astype(jnp.bfloat16)
        u_blocks = jnp.moveaxis(normed.reshape(SEQ_LEN, NB, block_width), 1, 0)
        gated_out = lax.map(mixer_block, (u_blocks, proj_in, tap_blocks, kernel_blocks))
        spread = jnp.transpose(gated_out.reshape(NB, SEQ_LEN, NB, sub_width), (1, 2, 0, 3)).reshape(SEQ_LEN, NB, block_width)
        mix_out = jnp.einsum('ljk,jkd->ljd', spread.astype(jnp.float32), proj_out.astype(jnp.float32), precision=upper_half)
        residual = (seq_float.reshape(SEQ_LEN, NB, block_width) + mix_out).astype(jnp.bfloat16).reshape(SEQ_LEN, D)
        finished = lax.map(mlp_rows, residual.reshape(8, SEQ_LEN // 8, D))
        return finished.reshape(SEQ_LEN, D)
    return lax.map(one_sequence, stream)
```

```python
import functools

import jax
import jax.numpy as jnp
from jax import lax
from jax.experimental import pallas as pl
from jax.experimental.pallas import tpu as pltpu
from jax.sharding import PartitionSpec as P

D = 1024
NB = 8
ROOT = 256
epsilon = 1e-05

f32 = jnp.float32
bf16 = jnp.bfloat16
VMEM_LIMIT = 56 * 1024 * 1024


def params():
    return pltpu.CompilerParams(vmem_limit_bytes=VMEM_LIMIT)


def column(row, width=128):
    return jnp.broadcast_to(row, (width, row.shape[1])).T


def wide(col, width):
    return jnp.concatenate([col] * (width // 128), axis=1)


def mixer_front(x_ref, sums_ref, rim_ref, gain_ref, proj_ref, taps_ref, fwd_ref, twid_ref, *rest):
    query_ref, *out_refs = rest[:-1]
    hist = rest[-1]
    step = pl.program_id(0)
    blocks, width, triple = proj_ref.shape
    rows = x_ref.shape[1]

    @pl.when(step == 0)
    def _():
        hist[:, 0:8, :] = rim_ref[0]

    scale = wide(column(lax.rsqrt(sums_ref[0] / D + epsilon)), blocks * width)
    normed = (x_ref[0].astype(f32) * scale * gain_ref[...]).astype(bf16)
    parts = []
    for b in range(blocks):
        proj = jnp.dot(normed[:, b * width : (b + 1) * width], proj_ref[b], preferred_element_type=f32)
        proj = proj.astype(bf16).astype(f32)
        hist[b, 8 : 8 + rows, :] = proj
        mixed = (
            taps_ref[0, b : b + 1] * proj
            + taps_ref[1, b : b + 1] * hist[b, 7 : 7 + rows, :]
            + taps_ref[2, b : b + 1] * hist[b, 6 : 6 + rows, :]
        )
        hist[b, 0:8, :] = hist[b, rows : rows + 8, :]
        query_ref[0, :, b * width : (b + 1) * width] = mixed[:, :width].astype(bf16)
        parts.append((mixed[:, width : 2 * width] * mixed[:, 2 * width :]).astype(bf16))
    source = jnp.concatenate(parts, axis=1)
    first = jnp.dot(fwd_ref[...], source, preferred_element_type=f32)
    first = (first * wide(column(twid_ref[0]), blocks * width)).astype(bf16)
    cols = out_refs[0].shape[1]
    for k, ref in enumerate(out_refs):
        ref[0] = first[k * cols : (k + 1) * cols]


def mixer_middle(count, *refs):
    ins = refs[:count]
    fwd_ref, kernel_ref, inv_ref, twid_ref = refs[count : count + 4]
    outs = refs[count + 4 : 2 * count + 4]
    held, done = refs[2 * count + 4 :]
    step = pl.program_id(0)
    rows, cols, width = ins[0].shape
    lanes = width // 128
    root = rows * count

    @pl.when(step == 0)
    def _():
        for k in range(count):
            for l in range(lanes):
                held[l, k * rows * cols : (k + 1) * rows * cols, :] = (
                    ins[k][:, :, l * 128 : (l + 1) * 128].astype(f32).reshape(rows * cols, 128)
                )

    table = jnp.concatenate(
        [held[l, pl.ds(step, root, stride=cols), :] for l in range(lanes)], axis=1
    ).astype(bf16)
    second = jnp.dot(fwd_ref[...], table, preferred_element_type=f32)
    second = (second * kernel_ref[0].astype(f32)).astype(bf16)
    third = jnp.dot(inv_ref[...], second, preferred_element_type=f32)
    third = third * wide(column(twid_ref[0]), width)
    for l in range(lanes):
        done[l, pl.ds(step, root, stride=cols), :] = third[:, l * 128 : (l + 1) * 128]

    @pl.when(step == cols - 1)
    def _():
        for k in range(count):
            for l in range(lanes):
                outs[k][:, :, l * 128 : (l + 1) * 128] = (
                    done[l, k * rows * cols : (k + 1) * rows * cols, :]
                    .astype(bf16)
                    .reshape(rows, cols, 128)
                )


def mixer_back(count, half, pos_ref, *refs):
    ins = refs[:count]
    inv_ref, query_ref, send_ref, own_ref = refs[count:]
    step = pl.program_id(0)
    table = jnp.concatenate([r[0] for r in ins], axis=0)
    conv = jnp.dot(inv_ref[...], table, preferred_element_type=f32)
    gated = (query_ref[0].astype(f32) * conv).astype(bf16)

    @pl.when(step < half)
    def _():
        send_ref[...] = gated

    @pl.when(step >= half)
    def _():
        own_ref[...] = gated


def mlp(pos_ref, own_ref, got_ref, x_own_ref, x_got_ref, mix_ref, gain_ref, up_ref, down_ref, *rest):
    out_ref, send_ref = rest[-2:]
    gated = jnp.concatenate([own_ref[...], got_ref[...]], axis=1)
    width = own_ref.shape[1]
    mix = jnp.dot(gated, mix_ref[...], preferred_element_type=f32)
    x = jnp.concatenate([x_own_ref[0], x_got_ref[...]], axis=1).astype(f32)
    resid = (x + mix).astype(bf16).astype(f32)
    sums = jnp.sum(resid * resid, axis=1, keepdims=True)
    normed = (resid * lax.rsqrt(sums / D + epsilon) * gain_ref[...]).astype(bf16)
    blocks, block, hidden = up_ref.shape
    acts = []
    for i in range(blocks):
        upper = jnp.dot(normed[:, i * block : (i + 1) * block], up_ref[i], preferred_element_type=f32)
        acts.append(jax.nn.gelu(upper).astype(bf16))
    pairs, _, span = down_ref.shape
    for p in range(pairs):
        act = jnp.concatenate([a[:, p * 128 : (p + 1) * 128] for a in acts], axis=1)
        low = jnp.dot(act, down_ref[p], preferred_element_type=f32)
        res = (resid[:, p * span : (p + 1) * span] + low).astype(bf16)
        if (p + 1) * span <= width:
            out_ref[0, :, p * span : (p + 1) * span] = res
        else:
            send_ref[:, p * span - width : (p + 1) * span - width] = res


def place(pos_ref, got_ref, _, out_ref):
    out_ref[0] = got_ref[...]


def body(
    stream,
    gain_mix,
    proj_in,
    short_taps,
    fwd_inner,
    twid_inner,
    fwd_outer,
    kernel,
    inv_outer,
    backward_twiddle,
    inv_inner,
    proj_out,
    gain_mlp,
    up_blocks,
    down_blocks,
):
    seqs, toks, width = stream.shape
    blocks, block = proj_in.shape[:2]
    root = fwd_inner.shape[0]
    rows = twid_inner.shape[0]
    cols = kernel.shape[1]
    count = lax.axis_size("ctx")
    sub = block // NB
    hidden = up_blocks.shape[2]
    hsub = hidden // NB
    half = rows // 2
    me = lax.axis_index("ctx")
    mp = lax.axis_index("mp")
    pos = jnp.stack([me, mp]).astype(jnp.int32)
    swap = [(0, 1), (1, 0)]

    order = me ^ jnp.arange(count)

    def relative(table):
        return jnp.take(
            table.reshape(count, root // count, -1), order, axis=0, mode="clip"
        ).reshape(root, -1)

    fwd_in = relative(fwd_inner.T)
    twid_in = relative(twid_inner.T).T.reshape(rows, 1, root)
    fwd_out = relative(fwd_outer).T
    inv_out = relative(inv_outer.T)
    twid_out = relative(backward_twiddle).T.reshape(cols, 1, root)
    inv_in = relative(inv_inner).T
    kernel_t = jnp.transpose(kernel, (1, 0, 2))

    def sumsq(x):
        x = x.astype(f32)
        part = jnp.sum(x * x, axis=-1)
        return part + lax.ppermute(part, "mp", swap)

    rim = lax.ppermute(stream[:, toks - 2 :], "ctx", [(i, i + 1) for i in range(count - 1)])
    sums = sumsq(stream).reshape(seqs, rows, 1, root)
    rim_norm = (
        rim.astype(f32) * lax.rsqrt(sumsq(rim)[..., None] / D + epsilon) * gain_mix.astype(f32)
    ).astype(bf16)
    rim_proj = jnp.einsum(
        "xtlc,lcd->xltd", rim_norm.reshape(seqs, 2, blocks, block), proj_in, preferred_element_type=f32
    )
    rim_proj = jnp.pad(rim_proj.astype(bf16).astype(f32), ((0, 0), (0, 0), (6, 0), (0, 0)))
    gain_in = gain_mix.astype(f32).reshape(1, width)

    def both(w):
        got = lax.ppermute(w, "mp", swap)
        return jnp.concatenate([w, got], axis=0)

    def by_source(w):
        n = w.shape[1] // 2
        return jnp.where(mp == 0, w, jnp.roll(w, n, axis=1))

    eye = jnp.eye(NB, dtype=bf16)
    out_tab = by_source(both(proj_out).reshape(NB, NB, sub, block))
    place_of = jnp.where(mp == 0, jnp.eye(NB, dtype=bf16), jnp.roll(jnp.eye(NB, dtype=bf16), NB // 2, axis=1))
    mix_tab = jnp.einsum("rj,ritd->ijtrd", place_of, out_tab).reshape(NB * block, NB * block)
    gain_out = both(gain_mlp).astype(f32).reshape(1, NB * block)
    up_tab = both(up_blocks)
    pair = 2
    pairs = NB // pair
    down_tab = by_source(both(down_blocks).reshape(NB, NB, hsub, block))
    down_tab = jnp.einsum(
        "pjitd,jk->pijtkd",
        down_tab.reshape(pairs, pair, NB, hsub, block),
        jnp.eye(pair, dtype=bf16),
    ).reshape(pairs, NB * pair * hsub, pair * block)
    up_tab = jnp.where(mp == 0, up_tab, jnp.roll(up_tab, hidden // 2, axis=2))

    def whole(array):
        return pl.BlockSpec(array.shape, lambda *_: (0,) * array.ndim)

    def swapped(parts):
        return [parts[0]] + [
            lax.ppermute(p, "ctx", [(i, i ^ k) for i in range(count)])
            for k, p in enumerate(parts)
            if k > 0
        ]

    piece = jax.ShapeDtypeStruct((rows, cols, width), bf16)

    def front(s):
        row_block = pl.BlockSpec((1, root, width), lambda i: (s, i, 0))
        return pl.pallas_call(
            mixer_front,
            grid=(rows,),
            in_specs=[
                row_block,
                pl.BlockSpec((1, 1, root), lambda i: (i, 0, 0)),
                pl.BlockSpec((1,) + rim_proj.shape[1:], lambda i: (s, 0, 0, 0)),
                whole(gain_in),
                whole(proj_in),
                whole(short_taps),
                whole(fwd_in),
                pl.BlockSpec((1, 1, root), lambda i: (i, 0, 0)),
            ],
            out_specs=[pl.BlockSpec((1, root, width), lambda i: (0, i, 0))]
            + [pl.BlockSpec((1, cols, width), lambda i: (i, 0, 0))] * count,
            out_shape=[jax.ShapeDtypeStruct((1, toks, width), bf16)] + [piece] * count,
            scratch_shapes=[pltpu.VMEM((blocks, root + 8, 3 * block), f32)],
            compiler_params=params(),
            name="mixer_front",
        )(stream, sums[s], rim_proj, gain_in, proj_in, short_taps, fwd_in, twid_in)

    def middle(parts):
        full = pl.BlockSpec((rows, cols, width), lambda i: (0, 0, 0))
        return pl.pallas_call(
            functools.partial(mixer_middle, count),
            grid=(cols,),
            in_specs=[full] * count
            + [
                whole(fwd_out),
                pl.BlockSpec((1, root, width), lambda i: (i, 0, 0)),
                whole(inv_out),
                pl.BlockSpec((1, 1, root), lambda i: (i, 0, 0)),
            ],
            out_specs=[full] * count,
            out_shape=[piece] * count,
            scratch_shapes=[pltpu.VMEM((width // 128, root * cols, 128), f32)] * 2,
            compiler_params=params(),
            name="mixer_middle",
        )(*parts, fwd_out, kernel_t, inv_out, twid_out)

    def back(parts, query):
        def row(i, pos):
            return lax.rem(i + half * (1 - pos[1]), rows)

        half_shape = jax.ShapeDtypeStruct((half * root, width), bf16)
        return pl.pallas_call(
            functools.partial(mixer_back, count, half),
            grid_spec=pltpu.PrefetchScalarGridSpec(
                num_scalar_prefetch=1,
                grid=(rows,),
                in_specs=[pl.BlockSpec((1, cols, width), lambda i, pos: (row(i, pos), 0, 0))] * count
                + [
                    whole(inv_in),
                    pl.BlockSpec((1, root, width), lambda i, pos: (0, row(i, pos), 0)),
                ],
                out_specs=[
                    pl.BlockSpec((root, width), lambda i, pos: (jnp.minimum(i, half - 1), 0)),
                    pl.BlockSpec((root, width), lambda i, pos: (jnp.maximum(i - half, 0), 0)),
                ],
            ),
            out_shape=[half_shape] * 2,
            compiler_params=params(),
            name="mixer_back",
        )(pos, *parts, inv_in, query)

    out_shape = jax.ShapeDtypeStruct(stream.shape, bf16)

    def channels(s, own, got, x_got, out):
        flat = pl.BlockSpec((root, width), lambda i, pos: (i, 0))
        mine = pl.BlockSpec((1, root, width), lambda i, pos: (s, pos[1] * half + i, 0))
        args = [pos, own, got, stream, x_got, mix_tab, gain_out, up_tab, down_tab]
        specs = [flat, flat, mine, flat, whole(mix_tab), whole(gain_out), whole(up_tab), whole(down_tab)]
        if out is not None:
            args.append(out)
            specs.append(pl.BlockSpec(memory_space=pl.ANY))
        return pl.pallas_call(
            mlp,
            grid_spec=pltpu.PrefetchScalarGridSpec(
                num_scalar_prefetch=1, grid=(half,), in_specs=specs, out_specs=[mine, flat]
            ),
            out_shape=[out_shape, jax.ShapeDtypeStruct((half * root, width), bf16)],
            input_output_aliases={} if out is None else {9: 0},
            compiler_params=params(),
            name="mlp",
        )(*args)

    def placed(s, got, out):
        return pl.pallas_call(
            place,
            grid_spec=pltpu.PrefetchScalarGridSpec(
                num_scalar_prefetch=1,
                grid=(2,),
                in_specs=[
                    pl.BlockSpec((half * root // 2, width), lambda i, pos: (i, 0)),
                    pl.BlockSpec(memory_space=pl.ANY),
                ],
                out_specs=pl.BlockSpec(
                    (1, half * root // 2, width), lambda i, pos: (s, (1 - pos[1]) * 2 + i, 0)
                ),
            ),
            out_shape=out_shape,
            input_output_aliases={2: 0},
            compiler_params=params(),
            name="place",
        )(pos, got, out)

    queries, firsts, x_gots = [], [], []
    for s in range(seqs):
        query, *parts = front(s)
        queries.append(query)
        firsts.append(swapped(parts))
        x_send = lax.dynamic_slice(stream, (s, (1 - mp) * (toks // 2), 0), (1, toks // 2, width))
        x_gots.append(lax.ppermute(x_send[0], "mp", swap))
    thirds = [swapped(middle(parts)) for parts in firsts]
    out = None
    waiting = []
    for s in range(seqs):
        send, own = back(thirds[s], queries[s])
        got = lax.ppermute(send, "mp", swap)
        out, send = channels(s, own, got, x_gots[s], out)
        waiting.append(lax.ppermute(send, "mp", swap))
        if s >= 1:
            out = placed(s - 1, waiting[s - 1], out)
    return placed(seqs - 1, waiting[seqs - 1], out)


def from_behind(array, axis, by):
    length = lax.axis_size(axis)
    pairs = [(i, i + by) for i in range(length) if 0 <= i + by < length]
    return lax.ppermute(array, axis, pairs)


def plain_body(
    stream,
    gain_mix,
    proj_in,
    short_taps,
    fwd_inner,
    twid_inner,
    fwd_outer,
    kernel,
    inv_outer,
    backward_twiddle,
    inv_inner,
    proj_out,
    gain_mlp,
    up_blocks,
    down_blocks,
):
    seq_count, tok_count, width_here = stream.shape
    blocks_here, block_width = (proj_in.shape[0], proj_in.shape[1])
    root_len = fwd_inner.shape[0]
    rows_here = twid_inner.shape[0]
    sub_width = block_width // NB
    hid_block = up_blocks.shape[2]
    hid_sub = hid_block // NB
    x_float = stream.astype(jnp.float32)
    sumsq_mix = lax.psum(jnp.sum(x_float * x_float, axis=2), "mp")
    normed = (
        x_float * lax.rsqrt(sumsq_mix[..., None] / D + epsilon) * gain_mix.astype(jnp.float32)
    ).astype(jnp.bfloat16)
    u_blocks = normed.reshape(seq_count, tok_count, blocks_here, block_width)
    projected = jnp.einsum(
        "xtlc,lcd->xtld", u_blocks, proj_in, preferred_element_type=jnp.float32
    ).astype(jnp.bfloat16)
    rim_rows = projected[:, tok_count - 2 :]
    earlier = from_behind(rim_rows, "ctx", 1)
    padded = jnp.concatenate([earlier, projected], axis=1).astype(jnp.float32)
    mixed_all = (
        short_taps[0] * padded[:, 2:]
        + short_taps[1] * padded[:, 1 : tok_count + 1]
        + short_taps[2] * padded[:, :tok_count]
    )
    query_part = mixed_all[..., :block_width].astype(jnp.bfloat16)
    source = (
        mixed_all[..., block_width : 2 * block_width] * mixed_all[..., 2 * block_width :]
    ).astype(jnp.bfloat16)
    lattice = source.reshape(seq_count, rows_here, root_len, blocks_here, block_width)
    opening_segment = (
        jnp.einsum("xablc,bf->xaflc", lattice, fwd_inner, preferred_element_type=jnp.float32)
        * twid_inner[None, :, :, None, None]
    ).astype(jnp.bfloat16)
    kernel_blocks = kernel.reshape(root_len, kernel.shape[1], blocks_here, block_width)
    middle_segment = (
        jnp.einsum(
            "xaflc,ag->xgflc",
            lax.all_to_all(opening_segment, "ctx", split_axis=2, concat_axis=1, tiled=True),
            fwd_outer,
            preferred_element_type=jnp.float32,
        )
        * kernel_blocks[None]
    ).astype(jnp.bfloat16)
    closing_segment = (
        jnp.einsum("xgflc,gh->xhflc", middle_segment, inv_outer, preferred_element_type=jnp.float32)
        * backward_twiddle[None, :, :, None, None]
    ).astype(jnp.bfloat16)
    returned = lax.all_to_all(closing_segment, "ctx", split_axis=1, concat_axis=2, tiled=True)
    convolved = jnp.einsum(
        "xhflc,fe->lcxhe", returned, inv_inner, preferred_element_type=jnp.float32
    ).reshape(blocks_here, block_width, seq_count, tok_count)
    gated_out = (jnp.transpose(query_part, (2, 3, 0, 1)).astype(jnp.float32) * convolved).astype(
        jnp.bfloat16
    )
    spread = gated_out.reshape(blocks_here, NB, sub_width, seq_count, tok_count)
    out_table = proj_out.reshape(blocks_here, NB, sub_width, block_width)
    mix_out = jnp.einsum(
        "ijtxs,jitd->xsjd",
        lax.all_to_all(spread, "mp", split_axis=1, concat_axis=0, tiled=True),
        out_table,
        preferred_element_type=jnp.float32,
    )
    residual = (x_float.reshape(seq_count, tok_count, blocks_here, block_width) + mix_out).astype(
        jnp.bfloat16
    )
    resid_float = residual.astype(jnp.float32)
    sumsq_mlp = lax.psum(jnp.sum(resid_float * resid_float, axis=(2, 3)), "mp")
    gain_here = gain_mlp.astype(jnp.float32).reshape(blocks_here, block_width)
    normed_mlp = (
        resid_float * lax.rsqrt(sumsq_mlp[..., None, None] / D + epsilon) * gain_here
    ).astype(jnp.bfloat16)
    upper_part = jnp.einsum(
        "xslc,lch->lhxs", normed_mlp, up_blocks, preferred_element_type=jnp.float32
    )
    active = (
        jax.nn.gelu(upper_part)
        .astype(jnp.bfloat16)
        .reshape(blocks_here, NB, hid_sub, seq_count, tok_count)
    )
    down_table = down_blocks.reshape(blocks_here, NB, hid_sub, block_width)
    lower_part = jnp.einsum(
        "ijtxs,jitd->xsjd",
        lax.all_to_all(active, "mp", split_axis=1, concat_axis=0, tiled=True),
        down_table,
        preferred_element_type=jnp.float32,
    )
    output = (
        (resid_float + lower_part).astype(jnp.bfloat16).reshape(seq_count, tok_count, width_here)
    )
    return output


def solution(mesh):
    placed = (
        P(None, "ctx", "mp"),
        P("mp"),
        P("mp", None, None),
        P(None, "mp", None),
        P(),
        P("ctx", None),
        P(),
        P(None, "ctx", "mp"),
        P(),
        P(None, "ctx"),
        P(),
        P("mp", None, None),
        P("mp"),
        P("mp", None, None),
        P("mp", None, None),
    )
    sizes = dict(mesh.shape)
    tiled = ROOT // sizes["ctx"] % 16 == 0 and sizes["mp"] == 2
    return jax.shard_map(
        body if tiled else plain_body, mesh=mesh, in_specs=placed, out_specs=P(None, "ctx", "mp"), check_vma=False
    )
```

```python
import functools

import jax
import jax.numpy as jnp
from jax import lax
from jax.experimental import pallas as pl
from jax.experimental.pallas import tpu as pltpu
from jax.sharding import PartitionSpec as P

D = 1024
NB = 8
ROOT = 256
epsilon = 1e-05

f32 = jnp.float32
bf16 = jnp.bfloat16
VMEM_LIMIT = 56 * 1024 * 1024


def params():
    return pltpu.CompilerParams(vmem_limit_bytes=VMEM_LIMIT)


def cost(us):
    return pl.CostEstimate(flops=0, bytes_accessed=int(us * 3.6e6), transcendentals=0)


def column(row, width=128):
    return jnp.broadcast_to(row, (width, row.shape[1])).T


def wide(col, width):
    return jnp.concatenate([col] * (width // 128), axis=1)


def mixer_front(extra, pos_ref, x_ref, sums_ref, rim_ref, gain_ref, proj_ref, taps_ref, fwd_ref, twid_ref, *rest):
    query_ref, across_ref, tail_ref, *out_refs = rest[extra:-1]
    hist = rest[-1]
    step = pl.program_id(0)
    blocks, width, triple = proj_ref.shape
    rows = x_ref.shape[1]

    @pl.when(step == 0)
    def _():
        hist[:, 0:8, :] = rim_ref[...]

    scale = wide(column(lax.rsqrt(sums_ref[0] / D + epsilon)), blocks * width)
    normed = (x_ref[0].astype(f32) * scale * gain_ref[...]).astype(bf16)
    parts = []
    for b in range(blocks):
        proj = jnp.dot(normed[:, b * width : (b + 1) * width], proj_ref[b], preferred_element_type=f32)
        proj = proj.astype(bf16).astype(f32)
        hist[b, 8 : 8 + rows, :] = proj
        mixed = (
            taps_ref[0, b : b + 1] * proj
            + taps_ref[1, b : b + 1] * hist[b, 7 : 7 + rows, :]
            + taps_ref[2, b : b + 1] * hist[b, 6 : 6 + rows, :]
        )
        hist[b, 0:8, :] = hist[b, rows : rows + 8, :]
        query_ref[0, :, b * width : (b + 1) * width] = mixed[:, :width].astype(bf16)
        parts.append((mixed[:, width : 2 * width] * mixed[:, 2 * width :]).astype(bf16))
    tail_ref[...] = hist[:, 0:8, :]

    @pl.when(lax.rem(step, 2) != pos_ref[1])
    def _():
        across_ref[...] = x_ref[0]

    source = jnp.concatenate(parts, axis=1)
    first = jnp.dot(fwd_ref[...], source, preferred_element_type=f32)
    first = (first * wide(column(twid_ref[0]), blocks * width)).astype(bf16)
    inner, _, cols, _ = out_refs[0].shape
    for k, ref in enumerate(out_refs):
        for j in range(inner):
            at = (k * inner + j) * cols
            ref[j, 0] = first[at : at + cols]


def regroup(count, *refs):
    ins = refs[:count]
    outs = refs[-(ins[0].shape[0] - 1) :]
    for q, out in enumerate(outs):
        for p in range(count):
            out[p] = ins[p][q + 1]


def mixer_middle(outer, inner, into, outof, *refs):
    count = outer * inner
    per = outer + inner - 1
    ins, refs = refs[: per * len(into)], refs[per * len(into) :]
    fwd_ref, kernel_ref, inv_ref, twid_ref = refs[:4]
    outs = refs[-2 - inner * len(outof) : -2]
    held, done = refs[-2:]
    step = pl.program_id(0)
    cols, width = ins[0].shape[-2:]
    lanes = width // 128
    root = fwd_ref.shape[0]
    rows = root // count

    @pl.when(step == 0)
    def _():
        for c, (start, size) in enumerate(into):
            for k in range(outer):
                for j in range(inner):
                    ref = ins[c * per + k].at[0] if j == 0 else ins[c * per + outer + j - 1].at[k]
                    at = ((k * inner + j) * rows + start) * cols
                    for l in range(lanes):
                        held[l, at : at + size * cols, :] = (
                            ref[:, :, l * 128 : (l + 1) * 128].astype(f32).reshape(size * cols, 128)
                        )

    table = jnp.concatenate(
        [held[l, pl.ds(step, root, stride=cols), :] for l in range(lanes)], axis=1
    ).astype(bf16)
    second = jnp.dot(fwd_ref[...], table, preferred_element_type=f32)
    second = (second * kernel_ref[0].astype(f32)).astype(bf16)
    third = jnp.dot(inv_ref[...], second, preferred_element_type=f32)
    third = third * wide(column(twid_ref[0]), width)
    for l in range(lanes):
        done[l, pl.ds(step, root, stride=cols), :] = third[:, l * 128 : (l + 1) * 128]

    @pl.when(step == cols - 1)
    def _():
        for c, (start, size) in enumerate(outof):
            for k in range(outer):
                for j in range(inner):
                    at = ((k * inner + j) * rows + 2 * start) * cols
                    for l in range(lanes):
                        outs[c * inner + j][k, :, :, l * 128 : (l + 1) * 128] = (
                            done[l, at : at + 2 * size * cols, :]
                            .astype(bf16)
                            .reshape(2 * size, cols, 128)
                        )


def mixer_back(outer, inner, half, pos_ref, *refs):
    ins = refs[: outer + inner - 1]
    inv_ref, query_ref = refs[outer + inner - 1 : outer + inner + 1]
    send_ref, own_ref = refs[-2:]
    step = pl.program_id(0)
    table = [r[0, 0] for r in ins[:inner]] + [r[j, 0] for r in ins[inner:] for j in range(inner)]
    table = jnp.concatenate(table, axis=0)
    conv = jnp.dot(inv_ref[...], table, preferred_element_type=f32)
    gated = (query_ref[0].astype(f32) * conv).astype(bf16)

    @pl.when(step < half)
    def _():
        send_ref[...] = gated

    @pl.when(step >= half)
    def _():
        own_ref[...] = gated


def mlp(pos_ref, own_ref, got_ref, x_own_ref, x_got_ref, mix_ref, gain_ref, up_ref, down_ref, *rest):
    out_ref, send_ref = rest[-2:]
    gated = jnp.concatenate([own_ref[...], got_ref[...]], axis=1)
    width = own_ref.shape[1]
    mix = jnp.dot(gated, mix_ref[...], preferred_element_type=f32)
    x = jnp.concatenate([x_own_ref[0], x_got_ref[...]], axis=1).astype(f32)
    resid = (x + mix).astype(bf16).astype(f32)
    sums = jnp.sum(resid * resid, axis=1, keepdims=True)
    normed = (resid * lax.rsqrt(sums / D + epsilon) * gain_ref[...]).astype(bf16)
    blocks, block, hidden = up_ref.shape
    acts = []
    for i in range(blocks):
        upper = jnp.dot(normed[:, i * block : (i + 1) * block], up_ref[i], preferred_element_type=f32)
        acts.append(jax.nn.gelu(upper).astype(bf16))
    pairs, _, span = down_ref.shape
    for p in range(pairs):
        act = jnp.concatenate([a[:, p * 128 : (p + 1) * 128] for a in acts], axis=1)
        low = jnp.dot(act, down_ref[p], preferred_element_type=f32)
        res = (resid[:, p * span : (p + 1) * span] + low).astype(bf16)
        if (p + 1) * span <= width:
            out_ref[0, :, p * span : (p + 1) * span] = res
        else:
            send_ref[:, p * span - width : (p + 1) * span - width] = res


def place(pos_ref, got_ref, *rest):
    rest[-1][0] = got_ref[...]


def body(
    stream,
    gain_mix,
    proj_in,
    short_taps,
    fwd_inner,
    twid_inner,
    fwd_outer,
    kernel,
    inv_outer,
    backward_twiddle,
    inv_inner,
    proj_out,
    gain_mlp,
    up_blocks,
    down_blocks,
):
    seqs, toks, width = stream.shape
    blocks, block = proj_in.shape[:2]
    root = fwd_inner.shape[0]
    rows = twid_inner.shape[0]
    cols = kernel.shape[1]
    count = lax.axis_size("ctx")
    sub = block // NB
    hidden = up_blocks.shape[2]
    hsub = hidden // NB
    half = rows // 2
    me = lax.axis_index("ctx")
    mp = lax.axis_index("mp")
    pos = jnp.stack([me, mp]).astype(jnp.int32)
    swap = [(0, 1), (1, 0)]

    inner = 4
    outer = count // inner
    legs = [0] + list(range(outer // 2, outer)) + list(range(1, outer // 2))
    turns = [k * inner + j for k in legs for j in range(inner)]
    order = me ^ jnp.array(turns, jnp.int32)

    def relative(table):
        return jnp.take(
            table.reshape(count, root // count, -1), order, axis=0, mode="clip"
        ).reshape(root, -1)

    fwd_in = relative(fwd_inner.T)
    twid_in = relative(twid_inner.T).T.reshape(rows, 1, root)
    fwd_out = relative(fwd_outer).T
    inv_out = relative(inv_outer.T)
    twid_out = relative(backward_twiddle).T.reshape(cols, 1, root)
    inv_in = relative(inv_inner).T
    kernel_t = jnp.transpose(kernel, (1, 0, 2))

    def sumsq(x):
        x = x.astype(f32)
        part = jnp.sum(x * x, axis=-1)
        return part + lax.ppermute(part, "mp", swap)

    rim = lax.ppermute(stream[:, toks - 2 :], "ctx", [(i, i + 1) for i in range(count - 1)])
    early, later = sumsq(stream[:1]), sumsq(stream[1:])
    sums = [(early[0] if s == 0 else later[s - 1]).reshape(rows, 1, root) for s in range(seqs)]
    rim_norm = (
        rim.astype(f32) * lax.rsqrt(sumsq(rim)[..., None] / D + epsilon) * gain_mix.astype(f32)
    ).astype(bf16)
    rim_proj = jnp.einsum(
        "xtlc,lcd->xltd", rim_norm.reshape(seqs, 2, blocks, block), proj_in, preferred_element_type=f32
    )
    rim_proj = jnp.pad(rim_proj.astype(bf16).astype(f32), ((0, 0), (0, 0), (6, 0), (0, 0)))
    gain_in = gain_mix.astype(f32).reshape(1, width)

    small = [proj_out, up_blocks, down_blocks, gain_mlp]
    packed = jnp.concatenate([w.reshape(-1, block) for w in small], axis=0)
    packed_got = lax.ppermute(packed, "mp", swap)

    def both(w):
        at = sum(v.size for v in small[: [v is w for v in small].index(True)]) // block
        got = packed_got[at : at + w.size // block].reshape(w.shape)
        return jnp.concatenate([w, got], axis=0)

    def by_source(w):
        n = w.shape[1] // 2
        return jnp.where(mp == 0, w, jnp.roll(w, n, axis=1))

    eye = jnp.eye(NB, dtype=bf16)
    out_tab = by_source(both(proj_out).reshape(NB, NB, sub, block))
    place_of = jnp.where(mp == 0, jnp.eye(NB, dtype=bf16), jnp.roll(jnp.eye(NB, dtype=bf16), NB // 2, axis=1))
    mix_tab = jnp.einsum("rj,ritd->ijtrd", place_of, out_tab).reshape(NB * block, NB * block)
    gain_out = both(gain_mlp).astype(f32).reshape(1, NB * block)
    up_tab = both(up_blocks)
    pair = 2
    pairs = NB // pair
    down_tab = by_source(both(down_blocks).reshape(NB, NB, hsub, block))
    down_tab = jnp.einsum(
        "pjitd,jk->pijtkd",
        down_tab.reshape(pairs, pair, NB, hsub, block),
        jnp.eye(pair, dtype=bf16),
    ).reshape(pairs, NB * pair * hsub, pair * block)
    up_tab = jnp.where(mp == 0, up_tab, jnp.roll(up_tab, hidden // 2, axis=2))

    def whole(array):
        return pl.BlockSpec(array.shape, lambda *_: (0,) * array.ndim)

    hbm = pl.BlockSpec(memory_space=pltpu.HBM)
    line = []

    def over(parts, shifts, note=False):
        got = [
            p if k == 0 else lax.ppermute(p, "ctx", [(i, i ^ k) for i in range(count)])
            for p, k in zip(parts, shifts)
        ]
        if note:
            line.extend(got[1:])
        return got

    def over_outer(parts):
        return over(parts, [k * inner for k in legs], True)

    def over_inner(parts):
        return over(parts, range(inner))

    def regrouped(parts, after):
        size = parts[0].shape[1]
        step = max(size // 4, 1)
        many = parts[0].shape[0] - 1
        shape = jax.ShapeDtypeStruct((len(parts),) + parts[0].shape[1:], bf16)

        def spec(n):
            return pl.BlockSpec((n, step, cols, width), lambda i: (0, i, 0, 0))

        return pl.pallas_call(
            functools.partial(regroup, len(parts)),
            grid=(size // step,),
            in_specs=[spec(many + 1)] * len(parts) + [hbm] * len(after),
            out_specs=[spec(len(parts))] * many,
            out_shape=[shape] * many,
            compiler_params=params(),
            cost_estimate=cost(4),
            name="regroup",
        )(*parts, *after)

    def front(s, start, size, rim, held, after):
        piece = jax.ShapeDtypeStruct((inner, size, cols, width), bf16)
        extra = list(after) + list(held)
        args = [pos, stream, sums[s], rim, gain_in, proj_in, short_taps, fwd_in, twid_in] + extra
        first = len(args) - 2
        query, across, tail, *parts = pl.pallas_call(
            functools.partial(mixer_front, len(extra)),
            grid_spec=pltpu.PrefetchScalarGridSpec(
                num_scalar_prefetch=1,
                grid=(size,),
                in_specs=[
                    pl.BlockSpec((1, root, width), lambda i, pos: (s, start + i, 0)),
                    pl.BlockSpec((1, 1, root), lambda i, pos: (start + i, 0, 0)),
                    whole(rim),
                    whole(gain_in),
                    whole(proj_in),
                    whole(short_taps),
                    whole(fwd_in),
                    pl.BlockSpec((1, 1, root), lambda i, pos: (start + i, 0, 0)),
                ]
                + [hbm] * len(extra),
                out_specs=[
                    pl.BlockSpec((1, root, width), lambda i, pos: (0, start + i, 0)),
                    pl.BlockSpec((root, width), lambda i, pos: ((start + i) // 2, 0)),
                    whole(rim),
                ]
                + [pl.BlockSpec((inner, 1, cols, width), lambda i, pos: (0, i, 0, 0))] * outer,
                scratch_shapes=[pltpu.VMEM((blocks, root + 8, 3 * block), f32)],
            ),
            out_shape=[
                jax.ShapeDtypeStruct((1, toks, width), bf16),
                jax.ShapeDtypeStruct((toks // 2, width), bf16),
                jax.ShapeDtypeStruct(rim.shape, f32),
            ]
            + [piece] * outer,
            input_output_aliases={first: 0, first + 1: 1} if held else {},
            compiler_params=params(),
            cost_estimate=cost(1.25 * size),
            name="mixer_front",
        )(*args)
        return (query, across), tail, parts

    def middle(pieces, into, outof, after):
        def specs(first, sizes):
            return [
                pl.BlockSpec((n,) + p, lambda i: (0, 0, 0, 0)) for p in sizes for n in first
            ]

        flat = [p for piece in pieces for p in piece]
        shapes = [(2 * n, cols, width) for _, n in outof]
        res = pl.pallas_call(
            functools.partial(mixer_middle, outer, inner, into, outof),
            grid=(cols,),
            in_specs=specs([1] * outer + [outer] * (inner - 1), [(n, cols, width) for _, n in into])
            + [
                whole(fwd_out),
                pl.BlockSpec((1, root, width), lambda i: (i, 0, 0)),
                whole(inv_out),
                pl.BlockSpec((1, 1, root), lambda i: (i, 0, 0)),
            ]
            + [hbm] * len(after),
            out_specs=specs([outer] * inner, shapes),
            out_shape=[jax.ShapeDtypeStruct((outer,) + p, bf16) for p in shapes for _ in range(inner)],
            scratch_shapes=[pltpu.VMEM((width // 128, root * cols, 128), f32)] * 2,
            compiler_params=params(),
            cost_estimate=cost(20),
            name="mixer_middle",
        )(*flat, fwd_out, kernel_t, inv_out, twid_out, *after)
        return [res[c * inner : (c + 1) * inner] for c in range(len(outof))]

    def back(parts, query, start, size, after):
        def local(i, pos):
            return jnp.where(i < size, 2 * i + 1 - pos[1], 2 * (i - size) + pos[1])

        def row(i, pos):
            return 2 * start + local(i, pos)

        shape = jax.ShapeDtypeStruct((size * root, width), bf16)
        return pl.pallas_call(
            functools.partial(mixer_back, outer, inner, size),
            grid_spec=pltpu.PrefetchScalarGridSpec(
                num_scalar_prefetch=1,
                grid=(2 * size,),
                in_specs=[pl.BlockSpec((1, 1, cols, width), lambda i, pos: (0, local(i, pos), 0, 0))] * inner
                + [pl.BlockSpec((inner, 1, cols, width), lambda i, pos: (0, local(i, pos), 0, 0))]
                * (outer - 1)
                + [
                    whole(inv_in),
                    pl.BlockSpec((1, root, width), lambda i, pos: (0, row(i, pos), 0)),
                ]
                + [hbm] * len(after),
                out_specs=[
                    pl.BlockSpec((root, width), lambda i, pos: (jnp.minimum(i, size - 1), 0)),
                    pl.BlockSpec((root, width), lambda i, pos: (jnp.maximum(i - size, 0), 0)),
                ],
            ),
            out_shape=[shape] * 2,
            compiler_params=params(),
            cost_estimate=cost(1.8 * size),
            name="mixer_back",
        )(pos, *parts, inv_in, query, *after)

    out_shape = jax.ShapeDtypeStruct(stream.shape, bf16)

    def channels(s, start, size, own, got, x_got, out, after):
        flat = pl.BlockSpec((root, width), lambda i, pos: (i, 0))
        mine = pl.BlockSpec((1, root, width), lambda i, pos: (s, 2 * (start + i) + pos[1], 0))
        theirs = pl.BlockSpec((root, width), lambda i, pos: (start + i, 0))
        args = [pos, own, got, stream, x_got, mix_tab, gain_out, up_tab, down_tab]
        specs = [flat, flat, mine, theirs, whole(mix_tab), whole(gain_out), whole(up_tab), whole(down_tab)]
        extra = list(after) + ([] if out is None else [out])
        args, specs = args + extra, specs + [hbm] * len(extra)
        return pl.pallas_call(
            mlp,
            grid_spec=pltpu.PrefetchScalarGridSpec(
                num_scalar_prefetch=1, grid=(size,), in_specs=specs, out_specs=[mine, flat]
            ),
            out_shape=[out_shape, jax.ShapeDtypeStruct((size * root, width), bf16)],
            input_output_aliases={} if out is None else {len(args) - 1: 0},
            compiler_params=params(),
            cost_estimate=cost(3.2 * size),
            name="mlp",
        )(*args)

    def placed(s, start, size, got, out):
        return pl.pallas_call(
            place,
            grid_spec=pltpu.PrefetchScalarGridSpec(
                num_scalar_prefetch=1,
                grid=(size,),
                in_specs=[pl.BlockSpec((root, width), lambda i, pos: (i, 0)), hbm],
                out_specs=pl.BlockSpec(
                    (1, root, width), lambda i, pos: (s, 2 * (start + i) + 1 - pos[1], 0)
                ),
            ),
            out_shape=out_shape,
            input_output_aliases={2: 0},
            compiler_params=params(),
            cost_estimate=cost(0.4 * size),
            name="place",
        )(pos, got, out)

    def cut(sizes):
        return [(sum(sizes[:i]), n) for i, n in enumerate(sizes)]

    into = [cut([half, half])] * seqs
    outof = [cut([half // 2, half // 2])] * seqs

    firsts, queries, thirds, x_gots, gates, sent = {}, {}, {}, {}, {}, {}
    out = None
    last = None

    def swap_x(a):
        return lax.ppermute(a, "mp", swap)

    def upto(n):
        return [] if n is None else line[max(n - 3, 0) : n]

    def do_front(s, c=0, n=None, extra=()):
        nonlocal last
        start, size = into[s][c]
        rim, held = (rim_proj[s], ()) if c == 0 else queries[s]
        held, rim, parts = front(
            s, start, size, rim, held, [*upto(n), *extra, *([] if last is None else [last])]
        )
        last = rim
        queries[s] = rim, held
        firsts[s, c] = parts
        if c + 1 == len(into[s]):
            x_gots[s] = swap_x(held[1])

    def do_go(s, c):
        firsts[s, c] = over_outer(firsts[s, c])

    def do_turn(s, c=0, n=None, extra=()):
        nonlocal last
        parts = firsts[s, c]
        res = regrouped(parts, [*upto(n), last, *extra])
        last = res[0]
        firsts[s, c] = parts + over_inner([None] + list(res))[1:]

    def do_middle(s, n=None, extra=()):
        nonlocal last
        pieces = [firsts[s, c] for c in range(len(into[s]))]
        res = middle(pieces, into[s], outof[s], [*upto(n), last, *extra])
        last = res[0][0]
        for c, parts in enumerate(res):
            thirds[s, c] = over_inner(parts)

    def do_return(s, c=0, n=None):
        nonlocal last
        parts = thirds[s, c]
        res = regrouped(parts, [*upto(n), last])
        last = res[0]
        thirds[s, c] = parts, res

    def do_send(s, c=0):
        parts, res = thirds[s, c]
        thirds[s, c] = parts + over_outer([None] + list(res))[1:]

    def do_back(s, c=0, n=None, extra=()):
        nonlocal last
        start, size = outof[s][c]
        send, own = back(thirds[s, c], queries[s][1][0], start, size, [*upto(n), last, *extra])
        last = own
        gates[s, c] = own, swap_x(send)

    def do_mlp(s, c=0, n=None, extra=()):
        nonlocal last, out
        start, size = outof[s][c]
        out, send = channels(s, start, size, *gates[s, c], x_gots[s], out, [*upto(n), last, *extra])
        last = send
        sent[s, c] = swap_x(send)

    def do_place(s, c=0):
        nonlocal out
        out = placed(s, *outof[s][c], sent[s, c], out)

    def at(groups):
        return int(groups * (outer - 1))

    do_front(0, 0)
    do_go(0, 0)
    do_front(0, 1)
    do_go(0, 1)
    do_front(1, 0, n=1)
    do_go(1, 0)
    do_front(1, 1, n=2)
    do_go(1, 1)
    do_turn(0, 0, n=3)
    do_front(2, 0, n=4)
    do_go(2, 0)
    do_front(2, 1, n=5)
    do_go(2, 1)
    do_turn(0, 1, n=6)
    do_middle(0, n=7, extra=[packed_got])
    do_front(3, 0, n=8)
    do_turn(1, 0, n=9)
    do_front(3, 1, n=10)
    do_return(0, 0, n=11)
    do_send(0, 0)
    do_return(0, 1, n=11)
    do_send(0, 1)
    do_go(3, 0)
    do_go(3, 1)
    do_turn(1, 1, n=12)
    do_middle(1, n=14, extra=[x_gots[0]])
    do_turn(2, 0, n=15)
    do_return(1, 0, n=16)
    do_send(1, 0)
    do_return(1, 1, n=17)
    do_send(1, 1)
    do_turn(2, 1, n=18)
    do_middle(2, n=20, extra=[x_gots[1]])
    do_back(0, 0, n=21)
    do_return(2, 0, n=22)
    do_send(2, 0)
    do_return(2, 1, n=23)
    do_send(2, 1)
    do_back(0, 1, n=24)
    do_mlp(0, 0, n=26)
    do_turn(3, 0, n=27, extra=[x_gots[2]])
    do_mlp(0, 1, n=29)
    do_turn(3, 1, n=30)
    do_middle(3, n=32)
    do_back(1, 0, n=33)
    do_place(0, 0)
    do_return(3, 0, n=34)
    do_send(3, 0)
    do_return(3, 1, n=35)
    do_send(3, 1)
    do_back(1, 1, n=36)
    do_mlp(1, 0, n=38, extra=[x_gots[3]])
    do_place(0, 1)
    do_back(2, 0, n=39)
    do_mlp(1, 1, n=41)
    do_place(1, 0)
    do_back(2, 1, n=42)
    do_mlp(2, 0, n=44)
    do_place(1, 1)
    do_back(3, 0, n=45)
    do_mlp(2, 1, n=47)
    do_back(3, 1)
    do_place(2, 0)
    do_mlp(3, 0)
    do_place(2, 1)
    do_mlp(3, 1)
    do_place(3, 0)
    do_place(3, 1)
    return out


def from_behind(array, axis, by):
    length = lax.axis_size(axis)
    pairs = [(i, i + by) for i in range(length) if 0 <= i + by < length]
    return lax.ppermute(array, axis, pairs)


def plain_body(
    stream,
    gain_mix,
    proj_in,
    short_taps,
    fwd_inner,
    twid_inner,
    fwd_outer,
    kernel,
    inv_outer,
    backward_twiddle,
    inv_inner,
    proj_out,
    gain_mlp,
    up_blocks,
    down_blocks,
):
    seq_count, tok_count, width_here = stream.shape
    blocks_here, block_width = (proj_in.shape[0], proj_in.shape[1])
    root_len = fwd_inner.shape[0]
    rows_here = twid_inner.shape[0]
    sub_width = block_width // NB
    hid_block = up_blocks.shape[2]
    hid_sub = hid_block // NB
    x_float = stream.astype(jnp.float32)
    sumsq_mix = lax.psum(jnp.sum(x_float * x_float, axis=2), "mp")
    normed = (
        x_float * lax.rsqrt(sumsq_mix[..., None] / D + epsilon) * gain_mix.astype(jnp.float32)
    ).astype(jnp.bfloat16)
    u_blocks = normed.reshape(seq_count, tok_count, blocks_here, block_width)
    projected = jnp.einsum(
        "xtlc,lcd->xtld", u_blocks, proj_in, preferred_element_type=jnp.float32
    ).astype(jnp.bfloat16)
    rim_rows = projected[:, tok_count - 2 :]
    earlier = from_behind(rim_rows, "ctx", 1)
    padded = jnp.concatenate([earlier, projected], axis=1).astype(jnp.float32)
    mixed_all = (
        short_taps[0] * padded[:, 2:]
        + short_taps[1] * padded[:, 1 : tok_count + 1]
        + short_taps[2] * padded[:, :tok_count]
    )
    query_part = mixed_all[..., :block_width].astype(jnp.bfloat16)
    source = (
        mixed_all[..., block_width : 2 * block_width] * mixed_all[..., 2 * block_width :]
    ).astype(jnp.bfloat16)
    lattice = source.reshape(seq_count, rows_here, root_len, blocks_here, block_width)
    opening_segment = (
        jnp.einsum("xablc,bf->xaflc", lattice, fwd_inner, preferred_element_type=jnp.float32)
        * twid_inner[None, :, :, None, None]
    ).astype(jnp.bfloat16)
    kernel_blocks = kernel.reshape(root_len, kernel.shape[1], blocks_here, block_width)
    middle_segment = (
        jnp.einsum(
            "xaflc,ag->xgflc",
            lax.all_to_all(opening_segment, "ctx", split_axis=2, concat_axis=1, tiled=True),
            fwd_outer,
            preferred_element_type=jnp.float32,
        )
        * kernel_blocks[None]
    ).astype(jnp.bfloat16)
    closing_segment = (
        jnp.einsum("xgflc,gh->xhflc", middle_segment, inv_outer, preferred_element_type=jnp.float32)
        * backward_twiddle[None, :, :, None, None]
    ).astype(jnp.bfloat16)
    returned = lax.all_to_all(closing_segment, "ctx", split_axis=1, concat_axis=2, tiled=True)
    convolved = jnp.einsum(
        "xhflc,fe->lcxhe", returned, inv_inner, preferred_element_type=jnp.float32
    ).reshape(blocks_here, block_width, seq_count, tok_count)
    gated_out = (jnp.transpose(query_part, (2, 3, 0, 1)).astype(jnp.float32) * convolved).astype(
        jnp.bfloat16
    )
    spread = gated_out.reshape(blocks_here, NB, sub_width, seq_count, tok_count)
    out_table = proj_out.reshape(blocks_here, NB, sub_width, block_width)
    mix_out = jnp.einsum(
        "ijtxs,jitd->xsjd",
        lax.all_to_all(spread, "mp", split_axis=1, concat_axis=0, tiled=True),
        out_table,
        preferred_element_type=jnp.float32,
    )
    residual = (x_float.reshape(seq_count, tok_count, blocks_here, block_width) + mix_out).astype(
        jnp.bfloat16
    )
    resid_float = residual.astype(jnp.float32)
    sumsq_mlp = lax.psum(jnp.sum(resid_float * resid_float, axis=(2, 3)), "mp")
    gain_here = gain_mlp.astype(jnp.float32).reshape(blocks_here, block_width)
    normed_mlp = (
        resid_float * lax.rsqrt(sumsq_mlp[..., None, None] / D + epsilon) * gain_here
    ).astype(jnp.bfloat16)
    upper_part = jnp.einsum(
        "xslc,lch->lhxs", normed_mlp, up_blocks, preferred_element_type=jnp.float32
    )
    active = (
        jax.nn.gelu(upper_part)
        .astype(jnp.bfloat16)
        .reshape(blocks_here, NB, hid_sub, seq_count, tok_count)
    )
    down_table = down_blocks.reshape(blocks_here, NB, hid_sub, block_width)
    lower_part = jnp.einsum(
        "ijtxs,jitd->xsjd",
        lax.all_to_all(active, "mp", split_axis=1, concat_axis=0, tiled=True),
        down_table,
        preferred_element_type=jnp.float32,
    )
    output = (
        (resid_float + lower_part).astype(jnp.bfloat16).reshape(seq_count, tok_count, width_here)
    )
    return output


def solution(mesh):
    placed = (
        P(None, "ctx", "mp"),
        P("mp"),
        P("mp", None, None),
        P(None, "mp", None),
        P(),
        P("ctx", None),
        P(),
        P(None, "ctx", "mp"),
        P(),
        P(None, "ctx"),
        P(),
        P("mp", None, None),
        P("mp"),
        P("mp", None, None),
        P("mp", None, None),
    )
    sizes = dict(mesh.shape)
    tiled = ROOT // sizes["ctx"] % 16 == 0 and sizes["mp"] == 2
    return jax.shard_map(
        body if tiled else plain_body, mesh=mesh, in_specs=placed, out_specs=P(None, "ctx", "mp"), check_vma=False
    )
```

```python
import functools

import jax
import jax.numpy as jnp
from jax import lax
from jax.experimental import pallas as pl
from jax.experimental.pallas import tpu as pltpu
from jax.sharding import PartitionSpec as P

D = 1024
NB = 8
ROOT = 256
epsilon = 1e-05

f32 = jnp.float32
bf16 = jnp.bfloat16
VMEM_LIMIT = 56 * 1024 * 1024


def params():
    return pltpu.CompilerParams(vmem_limit_bytes=VMEM_LIMIT)


def cost(us):
    return pl.CostEstimate(flops=0, bytes_accessed=int(us * 3.6e6), transcendentals=0)


def column(row, width=128):
    return jnp.broadcast_to(row, (width, row.shape[1])).T


def wide(col, width):
    return jnp.concatenate([col] * (width // 128), axis=1)


def mixer_front(extra, pos_ref, x_ref, sums_ref, rim_ref, gain_ref, proj_ref, taps_ref, fwd_ref, twid_ref, *rest):
    query_ref, across_ref, tail_ref, out_ref = rest[extra:-1]
    hist = rest[-1]
    step = pl.program_id(0)
    blocks, width, triple = proj_ref.shape
    rows = x_ref.shape[1]

    @pl.when(step == 0)
    def _():
        hist[:, 0:8, :] = rim_ref[...]

    scale = wide(column(lax.rsqrt(sums_ref[0] / D + epsilon)), blocks * width)
    normed = (x_ref[0].astype(f32) * scale * gain_ref[...]).astype(bf16)
    parts = []
    for b in range(blocks):
        proj = jnp.dot(normed[:, b * width : (b + 1) * width], proj_ref[b], preferred_element_type=f32)
        proj = proj.astype(bf16).astype(f32)
        hist[b, 8 : 8 + rows, :] = proj
        mixed = (
            taps_ref[0, b : b + 1] * proj
            + taps_ref[1, b : b + 1] * hist[b, 7 : 7 + rows, :]
            + taps_ref[2, b : b + 1] * hist[b, 6 : 6 + rows, :]
        )
        hist[b, 0:8, :] = hist[b, rows : rows + 8, :]
        query_ref[0, :, b * width : (b + 1) * width] = mixed[:, :width].astype(bf16)
        parts.append((mixed[:, width : 2 * width] * mixed[:, 2 * width :]).astype(bf16))
    tail_ref[...] = hist[:, 0:8, :]

    @pl.when(lax.rem(step, 2) != pos_ref[1])
    def _():
        across_ref[...] = x_ref[0]

    source = jnp.concatenate(parts, axis=1)
    first = jnp.dot(fwd_ref[...], source, preferred_element_type=f32)
    first = (first * wide(column(twid_ref[0]), blocks * width)).astype(bf16)
    out_ref[:, 0] = first.reshape(out_ref.shape[0], *out_ref.shape[2:])


def mixer_middle(into, outof, *refs):
    ins, refs = refs[: len(into)], refs[len(into) :]
    fwd_ref, kernel_ref, inv_ref, twid_ref = refs[:4]
    outs = refs[-2 - len(outof) : -2]
    held, done = refs[-2:]
    step = pl.program_id(0)
    count, _, cols, width = ins[0].shape
    lanes = width // 128
    root = fwd_ref.shape[0]
    rows = root // count

    @pl.when(step == 0)
    def _():
        for (start, size), ref in zip(into, ins):
            for k in range(count):
                at = (k * rows + start) * cols
                for l in range(lanes):
                    held[l, at : at + size * cols, :] = (
                        ref[k, :, :, l * 128 : (l + 1) * 128].astype(f32).reshape(size * cols, 128)
                    )

    table = jnp.concatenate(
        [held[l, pl.ds(step, root, stride=cols), :] for l in range(lanes)], axis=1
    ).astype(bf16)
    second = jnp.dot(fwd_ref[...], table, preferred_element_type=f32)
    second = (second * kernel_ref[0].astype(f32)).astype(bf16)
    third = jnp.dot(inv_ref[...], second, preferred_element_type=f32)
    third = third * wide(column(twid_ref[0]), width)
    for l in range(lanes):
        done[l, pl.ds(step, root, stride=cols), :] = third[:, l * 128 : (l + 1) * 128]

    @pl.when(step == cols - 1)
    def _():
        for (start, size), ref in zip(outof, outs):
            for k in range(count):
                at = (k * rows + 2 * start) * cols
                for l in range(lanes):
                    ref[k, :, :, l * 128 : (l + 1) * 128] = (
                        done[l, at : at + 2 * size * cols, :].astype(bf16).reshape(2 * size, cols, 128)
                    )


def mixer_back(half, pos_ref, in_ref, inv_ref, query_ref, *rest):
    send_ref, own_ref = rest[-2:]
    step = pl.program_id(0)
    table = in_ref[:, 0].reshape(inv_ref.shape[1], in_ref.shape[3])
    conv = jnp.dot(inv_ref[...], table, preferred_element_type=f32)
    gated = (query_ref[0].astype(f32) * conv).astype(bf16)

    @pl.when(step < half)
    def _():
        send_ref[...] = gated

    @pl.when(step >= half)
    def _():
        own_ref[...] = gated


def mlp(pos_ref, own_ref, got_ref, x_own_ref, x_got_ref, mix_ref, gain_ref, up_ref, down_ref, *rest):
    out_ref, send_ref = rest[-2:]
    gated = jnp.concatenate([own_ref[...], got_ref[...]], axis=1)
    width = own_ref.shape[1]
    mix = jnp.dot(gated, mix_ref[...], preferred_element_type=f32)
    x = jnp.concatenate([x_own_ref[0], x_got_ref[...]], axis=1).astype(f32)
    resid = (x + mix).astype(bf16).astype(f32)
    sums = jnp.sum(resid * resid, axis=1, keepdims=True)
    normed = (resid * lax.rsqrt(sums / D + epsilon) * gain_ref[...]).astype(bf16)
    blocks, block, hidden = up_ref.shape
    acts = []
    for i in range(blocks):
        upper = jnp.dot(normed[:, i * block : (i + 1) * block], up_ref[i], preferred_element_type=f32)
        acts.append(jax.nn.gelu(upper).astype(bf16))
    pairs, _, span = down_ref.shape
    for p in range(pairs):
        act = jnp.concatenate([a[:, p * 128 : (p + 1) * 128] for a in acts], axis=1)
        low = jnp.dot(act, down_ref[p], preferred_element_type=f32)
        res = (resid[:, p * span : (p + 1) * span] + low).astype(bf16)
        if (p + 1) * span <= width:
            out_ref[0, :, p * span : (p + 1) * span] = res
        else:
            send_ref[:, p * span - width : (p + 1) * span - width] = res


def hold(*refs):
    pass


def place(pos_ref, got_ref, *rest):
    rest[-1][0] = got_ref[...]


def body(
    stream,
    gain_mix,
    proj_in,
    short_taps,
    fwd_inner,
    twid_inner,
    fwd_outer,
    kernel,
    inv_outer,
    backward_twiddle,
    inv_inner,
    proj_out,
    gain_mlp,
    up_blocks,
    down_blocks,
):
    seqs, toks, width = stream.shape
    blocks, block = proj_in.shape[:2]
    root = fwd_inner.shape[0]
    rows = twid_inner.shape[0]
    cols = kernel.shape[1]
    count = lax.axis_size("ctx")
    sub = block // NB
    hidden = up_blocks.shape[2]
    hsub = hidden // NB
    half = rows // 2
    me = lax.axis_index("ctx")
    mp = lax.axis_index("mp")
    pos = jnp.stack([me, mp]).astype(jnp.int32)
    swap = [(0, 1), (1, 0)]

    fwd_in = fwd_inner.T
    twid_in = twid_inner.reshape(rows, 1, root)
    fwd_out = fwd_outer.T
    inv_out = inv_outer.T
    twid_out = backward_twiddle.T.reshape(cols, 1, root)
    inv_in = inv_inner.T
    kernel_t = jnp.transpose(kernel, (1, 0, 2))

    def sumsq(x):
        x = x.astype(f32)
        part = jnp.sum(x * x, axis=-1)
        return part + lax.ppermute(part, "mp", swap)

    ends = stream[:, toks - 2 :]
    rim = lax.ppermute(ends, "ctx", [(i, i + 1) for i in range(count - 1)])
    rim_other = lax.ppermute(
        ends, ("ctx", "mp"), [(2 * i + m, 2 * (i + 1) + 1 - m) for i in range(count - 1) for m in range(2)]
    )
    early, later = sumsq(stream[:1]), sumsq(stream[1:])
    sums = [(early[0] if s == 0 else later[s - 1]).reshape(rows, 1, root) for s in range(seqs)]
    rim_sums = jnp.sum(rim.astype(f32) ** 2, axis=-1) + jnp.sum(rim_other.astype(f32) ** 2, axis=-1)
    rim_norm = (
        rim.astype(f32) * lax.rsqrt(rim_sums[..., None] / D + epsilon) * gain_mix.astype(f32)
    ).astype(bf16)
    rim_proj = jnp.einsum(
        "xtlc,lcd->xltd", rim_norm.reshape(seqs, 2, blocks, block), proj_in, preferred_element_type=f32
    )
    rim_proj = jnp.pad(rim_proj.astype(bf16).astype(f32), ((0, 0), (0, 0), (6, 0), (0, 0)))
    gain_in = gain_mix.astype(f32).reshape(1, width)

    small = [proj_out, up_blocks, down_blocks, gain_mlp]
    packed = jnp.concatenate([w.reshape(-1, block) for w in small], axis=0)
    packed_got = lax.ppermute(packed, "mp", swap)

    def both(w):
        at = sum(v.size for v in small[: [v is w for v in small].index(True)]) // block
        got = packed_got[at : at + w.size // block].reshape(w.shape)
        return jnp.concatenate([w, got], axis=0)

    def by_source(w):
        n = w.shape[1] // 2
        return jnp.where(mp == 0, w, jnp.roll(w, n, axis=1))

    eye = jnp.eye(NB, dtype=bf16)
    out_tab = by_source(both(proj_out).reshape(NB, NB, sub, block))
    place_of = jnp.where(mp == 0, jnp.eye(NB, dtype=bf16), jnp.roll(jnp.eye(NB, dtype=bf16), NB // 2, axis=1))
    mix_tab = jnp.einsum("rj,ritd->ijtrd", place_of, out_tab).reshape(NB * block, NB * block)
    gain_out = both(gain_mlp).astype(f32).reshape(1, NB * block)
    up_tab = both(up_blocks)
    pair = 2
    pairs = NB // pair
    down_tab = by_source(both(down_blocks).reshape(NB, NB, hsub, block))
    down_tab = jnp.einsum(
        "pjitd,jk->pijtkd",
        down_tab.reshape(pairs, pair, NB, hsub, block),
        jnp.eye(pair, dtype=bf16),
    ).reshape(pairs, NB * pair * hsub, pair * block)
    up_tab = jnp.where(mp == 0, up_tab, jnp.roll(up_tab, hidden // 2, axis=2))

    def whole(array):
        return pl.BlockSpec(array.shape, lambda *_: (0,) * array.ndim)

    hbm = pl.BlockSpec(memory_space=pltpu.HBM)
    line = []

    def held_back(array, after):
        return pl.pallas_call(
            hold,
            in_specs=[hbm] * (1 + len(after)),
            out_specs=hbm,
            out_shape=jax.ShapeDtypeStruct(array.shape, array.dtype),
            input_output_aliases={0: 0},
            name="hold",
        )(array, *after)

    def exchanged(part, after=()):
        if after:
            part = held_back(part, after)
        line.append(lax.all_to_all(part, "ctx", 0, 0, tiled=True))
        return line[-1]

    def front(s, start, size, rim, held, after):
        piece = jax.ShapeDtypeStruct((count, size, cols, width), bf16)
        extra = list(after) + list(held)
        args = [pos, stream, sums[s], rim, gain_in, proj_in, short_taps, fwd_in, twid_in] + extra
        first = len(args) - 2
        query, across, tail, part = pl.pallas_call(
            functools.partial(mixer_front, len(extra)),
            grid_spec=pltpu.PrefetchScalarGridSpec(
                num_scalar_prefetch=1,
                grid=(size,),
                in_specs=[
                    pl.BlockSpec((1, root, width), lambda i, pos: (s, start + i, 0)),
                    pl.BlockSpec((1, 1, root), lambda i, pos: (start + i, 0, 0)),
                    whole(rim),
                    whole(gain_in),
                    whole(proj_in),
                    whole(short_taps),
                    whole(fwd_in),
                    pl.BlockSpec((1, 1, root), lambda i, pos: (start + i, 0, 0)),
                ]
                + [hbm] * len(extra),
                out_specs=[
                    pl.BlockSpec((1, root, width), lambda i, pos: (0, start + i, 0)),
                    pl.BlockSpec((root, width), lambda i, pos: ((start + i) // 2, 0)),
                    whole(rim),
                ]
                + [pl.BlockSpec((count, 1, cols, width), lambda i, pos: (0, i, 0, 0))],
                scratch_shapes=[pltpu.VMEM((blocks, root + 8, 3 * block), f32)],
            ),
            out_shape=[
                jax.ShapeDtypeStruct((1, toks, width), bf16),
                jax.ShapeDtypeStruct((toks // 2, width), bf16),
                jax.ShapeDtypeStruct(rim.shape, f32),
            ]
            + [piece],
            input_output_aliases={first: 0, first + 1: 1} if held else {},
            compiler_params=params(),
            cost_estimate=cost(1.25 * size),
            name="mixer_front",
        )(*args)
        return (query, across), tail, part

    def middle(pieces, into, outof, after):
        def fixed(n):
            return pl.BlockSpec((count, n, cols, width), lambda i: (0, 0, 0, 0))

        sizes = [2 * n for _, n in outof]
        return pl.pallas_call(
            functools.partial(mixer_middle, into, outof),
            grid=(cols,),
            in_specs=[fixed(n) for _, n in into]
            + [
                whole(fwd_out),
                pl.BlockSpec((1, root, width), lambda i: (i, 0, 0)),
                whole(inv_out),
                pl.BlockSpec((1, 1, root), lambda i: (i, 0, 0)),
            ]
            + [hbm] * len(after),
            out_specs=[fixed(n) for n in sizes],
            out_shape=[jax.ShapeDtypeStruct((count, n, cols, width), bf16) for n in sizes],
            scratch_shapes=[pltpu.VMEM((width // 128, root * cols, 128), f32)] * 2,
            compiler_params=params(),
            cost_estimate=cost(20),
            name="mixer_middle",
        )(*pieces, fwd_out, kernel_t, inv_out, twid_out, *after)

    def back(part, query, start, size, after):
        def local(i, pos):
            return jnp.where(i < size, 2 * i + 1 - pos[1], 2 * (i - size) + pos[1])

        def row(i, pos):
            return 2 * start + local(i, pos)

        shape = jax.ShapeDtypeStruct((size * root, width), bf16)
        return pl.pallas_call(
            functools.partial(mixer_back, size),
            grid_spec=pltpu.PrefetchScalarGridSpec(
                num_scalar_prefetch=1,
                grid=(2 * size,),
                in_specs=[pl.BlockSpec((count, 1, cols, width), lambda i, pos: (0, local(i, pos), 0, 0))]
                + [
                    whole(inv_in),
                    pl.BlockSpec((1, root, width), lambda i, pos: (0, row(i, pos), 0)),
                ]
                + [hbm] * len(after),
                out_specs=[
                    pl.BlockSpec((root, width), lambda i, pos: (jnp.minimum(i, size - 1), 0)),
                    pl.BlockSpec((root, width), lambda i, pos: (jnp.maximum(i - size, 0), 0)),
                ],
            ),
            out_shape=[shape] * 2,
            compiler_params=params(),
            cost_estimate=cost(1.8 * size),
            name="mixer_back",
        )(pos, part, inv_in, query, *after)

    out_shape = jax.ShapeDtypeStruct(stream.shape, bf16)

    def channels(s, start, size, own, got, x_got, out, after):
        flat = pl.BlockSpec((root, width), lambda i, pos: (i, 0))
        mine = pl.BlockSpec((1, root, width), lambda i, pos: (s, 2 * (start + i) + pos[1], 0))
        theirs = pl.BlockSpec((root, width), lambda i, pos: (start + i, 0))
        args = [pos, own, got, stream, x_got, mix_tab, gain_out, up_tab, down_tab]
        specs = [flat, flat, mine, theirs, whole(mix_tab), whole(gain_out), whole(up_tab), whole(down_tab)]
        extra = list(after) + ([] if out is None else [out])
        args, specs = args + extra, specs + [hbm] * len(extra)
        return pl.pallas_call(
            mlp,
            grid_spec=pltpu.PrefetchScalarGridSpec(
                num_scalar_prefetch=1, grid=(size,), in_specs=specs, out_specs=[mine, flat]
            ),
            out_shape=[out_shape, jax.ShapeDtypeStruct((size * root, width), bf16)],
            input_output_aliases={} if out is None else {len(args) - 1: 0},
            compiler_params=params(),
            cost_estimate=cost(3.2 * size),
            name="mlp",
        )(*args)

    def placed(s, start, size, got, out):
        return pl.pallas_call(
            place,
            grid_spec=pltpu.PrefetchScalarGridSpec(
                num_scalar_prefetch=1,
                grid=(size,),
                in_specs=[pl.BlockSpec((root, width), lambda i, pos: (i, 0)), hbm],
                out_specs=pl.BlockSpec(
                    (1, root, width), lambda i, pos: (s, 2 * (start + i) + 1 - pos[1], 0)
                ),
            ),
            out_shape=out_shape,
            input_output_aliases={2: 0},
            compiler_params=params(),
            cost_estimate=cost(0.4 * size),
            name="place",
        )(pos, got, out)

    def cut(sizes):
        return [(sum(sizes[:i]), n) for i, n in enumerate(sizes)]

    into = [cut([half, half])] + [cut([rows])] * (seqs - 1)
    outof = [cut([half])] * (seqs - 2) + [cut([half // 2, half // 2])] * 2

    firsts, queries, thirds, x_gots, gates, sent = {}, {}, {}, {}, {}, {}
    out = None
    last = None

    def swap_x(a):
        return lax.ppermute(a, "mp", swap)

    def upto(n):
        return line[n - 1 : n] if n else []

    def do_front(s, c=0, n=0, extra=()):
        nonlocal last
        start, size = into[s][c]
        rim, held = (rim_proj[s], ()) if c == 0 else queries[s]
        held, rim, part = front(
            s, start, size, rim, held, [*upto(n), *extra, *([] if last is None else [last])]
        )
        last = rim
        queries[s] = rim, held
        firsts[s, c] = part
        if c + 1 == len(into[s]):
            x_gots[s] = swap_x(held[1])

    def do_go(s, c=0, after=()):
        firsts[s, c] = exchanged(firsts[s, c], after)

    def do_middle(s, n=0, extra=()):
        nonlocal last
        pieces = [firsts[s, c] for c in range(len(into[s]))]
        res = middle(pieces, into[s], outof[s], [*upto(n), last, *extra])
        last = res[0]
        for c, part in enumerate(res):
            thirds[s, c] = part

    def do_send(s, c=0, after=()):
        thirds[s, c] = exchanged(thirds[s, c], after)

    def do_back(s, c=0, n=0, extra=()):
        nonlocal last
        start, size = outof[s][c]
        send, own = back(thirds[s, c], queries[s][1][0], start, size, [*upto(n), last, *extra])
        last = own
        gates[s, c] = own, swap_x(send)

    def do_mlp(s, c=0, n=0, extra=()):
        nonlocal last, out
        start, size = outof[s][c]
        out, send = channels(s, start, size, *gates[s, c], x_gots[s], out, [*upto(n), last, *extra])
        last = send
        sent[s, c] = swap_x(send)

    def do_place(s, c=0):
        nonlocal out
        out = placed(s, *outof[s][c], sent[s, c], out)

    do_front(0, 0)
    do_go(0, 0)
    do_front(0, 1, extra=[sums[1]])
    do_go(0, 1)
    do_front(1, n=1)
    do_go(1, 0, [x_gots[0]])
    do_middle(0, n=2)
    do_front(2, n=2)
    do_send(0, 0, [last, x_gots[1]])
    do_middle(1, n=3)
    do_front(3, n=3)
    do_send(1, 0, [last, x_gots[2]])
    do_back(0, n=4)
    do_go(2, 0, [last, x_gots[3], packed_got])
    do_back(1, n=5)
    do_mlp(0, n=5)
    do_go(3, 0, [last, gates[1, 0][1]])
    do_middle(2, n=6)
    do_mlp(1, n=6)
    do_send(2, 0, [last, sent[0, 0]])
    do_middle(3, n=7)
    do_send(2, 1, [last, sent[1, 0]])
    do_back(2, 0, n=8)
    do_place(0)
    do_send(3, 0, [last, gates[2, 0][1]])
    do_back(2, 1, n=9)
    do_mlp(2, 0, n=9)
    do_send(3, 1, [last, gates[2, 1][1]])
    do_back(3, 0, n=10)
    do_mlp(2, 1, n=10)
    do_place(1)
    do_back(3, 1)
    do_mlp(3, 0)
    do_place(2, 0)
    do_place(2, 1)
    do_mlp(3, 1)
    do_place(3, 0)
    do_place(3, 1)
    return out


def from_behind(array, axis, by):
    length = lax.axis_size(axis)
    pairs = [(i, i + by) for i in range(length) if 0 <= i + by < length]
    return lax.ppermute(array, axis, pairs)


def plain_body(
    stream,
    gain_mix,
    proj_in,
    short_taps,
    fwd_inner,
    twid_inner,
    fwd_outer,
    kernel,
    inv_outer,
    backward_twiddle,
    inv_inner,
    proj_out,
    gain_mlp,
    up_blocks,
    down_blocks,
):
    seq_count, tok_count, width_here = stream.shape
    blocks_here, block_width = (proj_in.shape[0], proj_in.shape[1])
    root_len = fwd_inner.shape[0]
    rows_here = twid_inner.shape[0]
    sub_width = block_width // NB
    hid_block = up_blocks.shape[2]
    hid_sub = hid_block // NB
    x_float = stream.astype(jnp.float32)
    sumsq_mix = lax.psum(jnp.sum(x_float * x_float, axis=2), "mp")
    normed = (
        x_float * lax.rsqrt(sumsq_mix[..., None] / D + epsilon) * gain_mix.astype(jnp.float32)
    ).astype(jnp.bfloat16)
    u_blocks = normed.reshape(seq_count, tok_count, blocks_here, block_width)
    projected = jnp.einsum(
        "xtlc,lcd->xtld", u_blocks, proj_in, preferred_element_type=jnp.float32
    ).astype(jnp.bfloat16)
    rim_rows = projected[:, tok_count - 2 :]
    earlier = from_behind(rim_rows, "ctx", 1)
    padded = jnp.concatenate([earlier, projected], axis=1).astype(jnp.float32)
    mixed_all = (
        short_taps[0] * padded[:, 2:]
        + short_taps[1] * padded[:, 1 : tok_count + 1]
        + short_taps[2] * padded[:, :tok_count]
    )
    query_part = mixed_all[..., :block_width].astype(jnp.bfloat16)
    source = (
        mixed_all[..., block_width : 2 * block_width] * mixed_all[..., 2 * block_width :]
    ).astype(jnp.bfloat16)
    lattice = source.reshape(seq_count, rows_here, root_len, blocks_here, block_width)
    opening_segment = (
        jnp.einsum("xablc,bf->xaflc", lattice, fwd_inner, preferred_element_type=jnp.float32)
        * twid_inner[None, :, :, None, None]
    ).astype(jnp.bfloat16)
    kernel_blocks = kernel.reshape(root_len, kernel.shape[1], blocks_here, block_width)
    middle_segment = (
        jnp.einsum(
            "xaflc,ag->xgflc",
            lax.all_to_all(opening_segment, "ctx", split_axis=2, concat_axis=1, tiled=True),
            fwd_outer,
            preferred_element_type=jnp.float32,
        )
        * kernel_blocks[None]
    ).astype(jnp.bfloat16)
    closing_segment = (
        jnp.einsum("xgflc,gh->xhflc", middle_segment, inv_outer, preferred_element_type=jnp.float32)
        * backward_twiddle[None, :, :, None, None]
    ).astype(jnp.bfloat16)
    returned = lax.all_to_all(closing_segment, "ctx", split_axis=1, concat_axis=2, tiled=True)
    convolved = jnp.einsum(
        "xhflc,fe->lcxhe", returned, inv_inner, preferred_element_type=jnp.float32
    ).reshape(blocks_here, block_width, seq_count, tok_count)
    gated_out = (jnp.transpose(query_part, (2, 3, 0, 1)).astype(jnp.float32) * convolved).astype(
        jnp.bfloat16
    )
    spread = gated_out.reshape(blocks_here, NB, sub_width, seq_count, tok_count)
    out_table = proj_out.reshape(blocks_here, NB, sub_width, block_width)
    mix_out = jnp.einsum(
        "ijtxs,jitd->xsjd",
        lax.all_to_all(spread, "mp", split_axis=1, concat_axis=0, tiled=True),
        out_table,
        preferred_element_type=jnp.float32,
    )
    residual = (x_float.reshape(seq_count, tok_count, blocks_here, block_width) + mix_out).astype(
        jnp.bfloat16
    )
    resid_float = residual.astype(jnp.float32)
    sumsq_mlp = lax.psum(jnp.sum(resid_float * resid_float, axis=(2, 3)), "mp")
    gain_here = gain_mlp.astype(jnp.float32).reshape(blocks_here, block_width)
    normed_mlp = (
        resid_float * lax.rsqrt(sumsq_mlp[..., None, None] / D + epsilon) * gain_here
    ).astype(jnp.bfloat16)
    upper_part = jnp.einsum(
        "xslc,lch->lhxs", normed_mlp, up_blocks, preferred_element_type=jnp.float32
    )
    active = (
        jax.nn.gelu(upper_part)
        .astype(jnp.bfloat16)
        .reshape(blocks_here, NB, hid_sub, seq_count, tok_count)
    )
    down_table = down_blocks.reshape(blocks_here, NB, hid_sub, block_width)
    lower_part = jnp.einsum(
        "ijtxs,jitd->xsjd",
        lax.all_to_all(active, "mp", split_axis=1, concat_axis=0, tiled=True),
        down_table,
        preferred_element_type=jnp.float32,
    )
    output = (
        (resid_float + lower_part).astype(jnp.bfloat16).reshape(seq_count, tok_count, width_here)
    )
    return output


def solution(mesh):
    placed = (
        P(None, "ctx", "mp"),
        P("mp"),
        P("mp", None, None),
        P(None, "mp", None),
        P(),
        P("ctx", None),
        P(),
        P(None, "ctx", "mp"),
        P(),
        P(None, "ctx"),
        P(),
        P("mp", None, None),
        P("mp"),
        P("mp", None, None),
        P("mp", None, None),
    )
    sizes = dict(mesh.shape)
    tiled = ROOT // sizes["ctx"] % 16 == 0 and sizes["mp"] == 2
    return jax.shard_map(
        body if tiled else plain_body, mesh=mesh, in_specs=placed, out_specs=P(None, "ctx", "mp"), check_vma=False
    )
```

```python
import functools

import jax
import jax.numpy as jnp
from jax import lax
from jax.experimental import pallas as pl
from jax.experimental.pallas import tpu as pltpu
from jax.sharding import PartitionSpec as P

D = 1024
NB = 8
ROOT = 256
epsilon = 1e-05

f32 = jnp.float32
bf16 = jnp.bfloat16
VMEM_LIMIT = 56 * 1024 * 1024


def params():
    return pltpu.CompilerParams(vmem_limit_bytes=VMEM_LIMIT)


def cost(us):
    return pl.CostEstimate(flops=0, bytes_accessed=int(us * 3.6e6), transcendentals=0)


def column(row, width=128):
    return jnp.broadcast_to(row, (width, row.shape[1])).T


def wide(col, width):
    return jnp.concatenate([col] * (width // 128), axis=1)


def mixer_front(extra, pos_ref, x_ref, sums_ref, rim_ref, gain_ref, proj_ref, taps_ref, fwd_ref, twid_ref, *rest):
    query_ref, across_ref, tail_ref, out_ref = rest[extra:-1]
    hist = rest[-1]
    step = pl.program_id(0)
    blocks, width, triple = proj_ref.shape
    rows = x_ref.shape[1]

    @pl.when(step == 0)
    def _():
        hist[:, 0:8, :] = rim_ref[...]

    scale = wide(column(lax.rsqrt(sums_ref[0] / D + epsilon)), blocks * width)
    normed = (x_ref[0].astype(f32) * scale * gain_ref[...]).astype(bf16)
    parts = []
    for b in range(blocks):
        proj = jnp.dot(normed[:, b * width : (b + 1) * width], proj_ref[b], preferred_element_type=f32)
        proj = proj.astype(bf16).astype(f32)
        hist[b, 8 : 8 + rows, :] = proj
        mixed = (
            taps_ref[0, b : b + 1] * proj
            + taps_ref[1, b : b + 1] * hist[b, 7 : 7 + rows, :]
            + taps_ref[2, b : b + 1] * hist[b, 6 : 6 + rows, :]
        )
        hist[b, 0:8, :] = hist[b, rows : rows + 8, :]
        query_ref[0, :, b * width : (b + 1) * width] = mixed[:, :width].astype(bf16)
        parts.append((mixed[:, width : 2 * width] * mixed[:, 2 * width :]).astype(bf16))
    tail_ref[...] = hist[:, 0:8, :]

    @pl.when(lax.rem(step, 2) != pos_ref[1])
    def _():
        across_ref[...] = x_ref[0]

    source = jnp.concatenate(parts, axis=1)
    first = jnp.dot(fwd_ref[...], source, preferred_element_type=f32)
    first = (first * wide(column(twid_ref[0]), blocks * width)).astype(bf16)
    out_ref[:, 0] = first.reshape(out_ref.shape[0], *out_ref.shape[2:])


def mixer_middle(into, outof, *refs):
    ins, refs = refs[: len(into)], refs[len(into) :]
    fwd_ref, kernel_ref, inv_ref, twid_ref = refs[:4]
    outs = refs[-2 - len(outof) : -2]
    held, done = refs[-2:]
    step = pl.program_id(0)
    count, _, cols, width = ins[0].shape
    lanes = width // 128
    root = fwd_ref.shape[0]
    rows = root // count

    @pl.when(step == 0)
    def _():
        for (start, size), ref in zip(into, ins):
            for k in range(count):
                at = (k * rows + start) * cols
                for l in range(lanes):
                    held[l, at : at + size * cols, :] = (
                        ref[k, :, :, l * 128 : (l + 1) * 128].astype(f32).reshape(size * cols, 128)
                    )

    table = jnp.concatenate(
        [held[l, pl.ds(step, root, stride=cols), :] for l in range(lanes)], axis=1
    ).astype(bf16)
    second = jnp.dot(fwd_ref[...], table, preferred_element_type=f32)
    second = (second * kernel_ref[0].astype(f32)).astype(bf16)
    third = jnp.dot(inv_ref[...], second, preferred_element_type=f32)
    third = third * wide(column(twid_ref[0]), width)
    for l in range(lanes):
        done[l, pl.ds(step, root, stride=cols), :] = third[:, l * 128 : (l + 1) * 128]

    @pl.when(step == cols - 1)
    def _():
        for (start, size), ref in zip(outof, outs):
            for k in range(count):
                at = (k * rows + 2 * start) * cols
                for l in range(lanes):
                    ref[k, :, :, l * 128 : (l + 1) * 128] = (
                        done[l, at : at + 2 * size * cols, :].astype(bf16).reshape(2 * size, cols, 128)
                    )


def mixer_back(half, pos_ref, in_ref, inv_ref, query_ref, *rest):
    send_ref, own_ref = rest[-2:]
    step = pl.program_id(0)
    table = in_ref[:, 0].reshape(inv_ref.shape[1], in_ref.shape[3])
    conv = jnp.dot(inv_ref[...], table, preferred_element_type=f32)
    gated = (query_ref[0].astype(f32) * conv).astype(bf16)

    @pl.when(step < half)
    def _():
        send_ref[...] = gated

    @pl.when(step >= half)
    def _():
        own_ref[...] = gated


def mlp(pos_ref, own_ref, got_ref, x_own_ref, x_got_ref, mix_ref, gain_ref, up_ref, down_ref, *rest):
    out_ref, send_ref = rest[-2:]
    gated = jnp.concatenate([own_ref[...], got_ref[...]], axis=1)
    width = own_ref.shape[1]
    mix = jnp.dot(gated, mix_ref[...], preferred_element_type=f32)
    x = jnp.concatenate([x_own_ref[0], x_got_ref[...]], axis=1).astype(f32)
    resid = (x + mix).astype(bf16).astype(f32)
    sums = jnp.sum(resid * resid, axis=1, keepdims=True)
    normed = (resid * lax.rsqrt(sums / D + epsilon) * gain_ref[...]).astype(bf16)
    blocks, block, hidden = up_ref.shape
    acts = []
    for i in range(blocks):
        upper = jnp.dot(normed[:, i * block : (i + 1) * block], up_ref[i], preferred_element_type=f32)
        acts.append(jax.nn.gelu(upper).astype(bf16))
    pairs, _, span = down_ref.shape
    for p in range(pairs):
        act = jnp.concatenate([a[:, p * 128 : (p + 1) * 128] for a in acts], axis=1)
        low = jnp.dot(act, down_ref[p], preferred_element_type=f32)
        res = (resid[:, p * span : (p + 1) * span] + low).astype(bf16)
        if (p + 1) * span <= width:
            out_ref[0, :, p * span : (p + 1) * span] = res
        else:
            send_ref[:, p * span - width : (p + 1) * span - width] = res


def hold(*refs):
    pass


def place(pos_ref, got_ref, *rest):
    rest[-1][0] = got_ref[...]


def body(
    stream,
    gain_mix,
    proj_in,
    short_taps,
    fwd_inner,
    twid_inner,
    fwd_outer,
    kernel,
    inv_outer,
    backward_twiddle,
    inv_inner,
    proj_out,
    gain_mlp,
    up_blocks,
    down_blocks,
):
    seqs, toks, width = stream.shape
    blocks, block = proj_in.shape[:2]
    root = fwd_inner.shape[0]
    rows = twid_inner.shape[0]
    cols = kernel.shape[1]
    count = lax.axis_size("ctx")
    sub = block // NB
    hidden = up_blocks.shape[2]
    hsub = hidden // NB
    half = rows // 2
    me = lax.axis_index("ctx")
    mp = lax.axis_index("mp")
    pos = jnp.stack([me, mp]).astype(jnp.int32)
    swap = [(0, 1), (1, 0)]

    fwd_in = fwd_inner.T
    twid_in = twid_inner.reshape(rows, 1, root)
    fwd_out = fwd_outer.T
    inv_out = inv_outer.T
    twid_out = backward_twiddle.T.reshape(cols, 1, root)
    inv_in = inv_inner.T
    kernel_t = jnp.transpose(kernel, (1, 0, 2))

    def sumsq(x):
        x = x.astype(f32)
        part = jnp.sum(x * x, axis=-1)
        return part + lax.ppermute(part, "mp", swap)

    ends = stream[:, toks - 2 :]
    rim = lax.ppermute(ends, "ctx", [(i, i + 1) for i in range(count - 1)])
    rim_other = lax.ppermute(
        ends, ("ctx", "mp"), [(2 * i + m, 2 * (i + 1) + 1 - m) for i in range(count - 1) for m in range(2)]
    )
    early, later = sumsq(stream[:1]), sumsq(stream[1:])
    sums = [(early[0] if s == 0 else later[s - 1]).reshape(rows, 1, root) for s in range(seqs)]
    rim_sums = jnp.sum(rim.astype(f32) ** 2, axis=-1) + jnp.sum(rim_other.astype(f32) ** 2, axis=-1)
    rim_norm = (
        rim.astype(f32) * lax.rsqrt(rim_sums[..., None] / D + epsilon) * gain_mix.astype(f32)
    ).astype(bf16)
    rim_proj = jnp.einsum(
        "xtlc,lcd->xltd", rim_norm.reshape(seqs, 2, blocks, block), proj_in, preferred_element_type=f32
    )
    rim_proj = jnp.pad(rim_proj.astype(bf16).astype(f32), ((0, 0), (0, 0), (6, 0), (0, 0)))
    gain_in = gain_mix.astype(f32).reshape(1, width)

    small = [proj_out, up_blocks, down_blocks, gain_mlp]
    packed = jnp.concatenate([w.reshape(-1, block) for w in small], axis=0)
    packed_got = lax.ppermute(packed, "mp", swap)

    def both(w):
        at = sum(v.size for v in small[: [v is w for v in small].index(True)]) // block
        got = packed_got[at : at + w.size // block].reshape(w.shape)
        return jnp.concatenate([w, got], axis=0)

    def by_source(w):
        n = w.shape[1] // 2
        return jnp.where(mp == 0, w, jnp.roll(w, n, axis=1))

    eye = jnp.eye(NB, dtype=bf16)
    out_tab = by_source(both(proj_out).reshape(NB, NB, sub, block))
    place_of = jnp.where(mp == 0, jnp.eye(NB, dtype=bf16), jnp.roll(jnp.eye(NB, dtype=bf16), NB // 2, axis=1))
    mix_tab = jnp.einsum("rj,ritd->ijtrd", place_of, out_tab).reshape(NB * block, NB * block)
    gain_out = both(gain_mlp).astype(f32).reshape(1, NB * block)
    up_tab = both(up_blocks)
    pair = 2
    pairs = NB // pair
    down_tab = by_source(both(down_blocks).reshape(NB, NB, hsub, block))
    down_tab = jnp.einsum(
        "pjitd,jk->pijtkd",
        down_tab.reshape(pairs, pair, NB, hsub, block),
        jnp.eye(pair, dtype=bf16),
    ).reshape(pairs, NB * pair * hsub, pair * block)
    up_tab = jnp.where(mp == 0, up_tab, jnp.roll(up_tab, hidden // 2, axis=2))

    def whole(array):
        return pl.BlockSpec(array.shape, lambda *_: (0,) * array.ndim)

    hbm = pl.BlockSpec(memory_space=pltpu.HBM)
    line = []

    def held_back(array, after):
        return pl.pallas_call(
            hold,
            in_specs=[hbm] * (1 + len(after)),
            out_specs=hbm,
            out_shape=jax.ShapeDtypeStruct(array.shape, array.dtype),
            input_output_aliases={0: 0},
            name="hold",
        )(array, *after)

    def exchanged(part, after=()):
        if after:
            part = held_back(part, after)
        line.append(lax.all_to_all(part, "ctx", 0, 0, tiled=True))
        return line[-1]

    def front(s, start, size, rim, held, after):
        piece = jax.ShapeDtypeStruct((count, size, cols, width), bf16)
        extra = list(after) + list(held)
        args = [pos, stream, sums[s], rim, gain_in, proj_in, short_taps, fwd_in, twid_in] + extra
        first = len(args) - 2
        query, across, tail, part = pl.pallas_call(
            functools.partial(mixer_front, len(extra)),
            grid_spec=pltpu.PrefetchScalarGridSpec(
                num_scalar_prefetch=1,
                grid=(size,),
                in_specs=[
                    pl.BlockSpec((1, root, width), lambda i, pos: (s, start + i, 0)),
                    pl.BlockSpec((1, 1, root), lambda i, pos: (start + i, 0, 0)),
                    whole(rim),
                    whole(gain_in),
                    whole(proj_in),
                    whole(short_taps),
                    whole(fwd_in),
                    pl.BlockSpec((1, 1, root), lambda i, pos: (start + i, 0, 0)),
                ]
                + [hbm] * len(extra),
                out_specs=[
                    pl.BlockSpec((1, root, width), lambda i, pos: (0, start + i, 0)),
                    pl.BlockSpec((root, width), lambda i, pos: ((start + i) // 2, 0)),
                    whole(rim),
                ]
                + [pl.BlockSpec((count, 1, cols, width), lambda i, pos: (0, i, 0, 0))],
                scratch_shapes=[pltpu.VMEM((blocks, root + 8, 3 * block), f32)],
            ),
            out_shape=[
                jax.ShapeDtypeStruct((1, toks, width), bf16),
                jax.ShapeDtypeStruct((toks // 2, width), bf16),
                jax.ShapeDtypeStruct(rim.shape, f32),
            ]
            + [piece],
            input_output_aliases={first: 0, first + 1: 1} if held else {},
            compiler_params=params(),
            cost_estimate=cost(1.25 * size),
            name="mixer_front",
        )(*args)
        return (query, across), tail, part

    def middle(pieces, into, outof, after):
        def fixed(n):
            return pl.BlockSpec((count, n, cols, width), lambda i: (0, 0, 0, 0))

        sizes = [2 * n for _, n in outof]
        return pl.pallas_call(
            functools.partial(mixer_middle, into, outof),
            grid=(cols,),
            in_specs=[fixed(n) for _, n in into]
            + [
                whole(fwd_out),
                pl.BlockSpec((1, root, width), lambda i: (i, 0, 0)),
                whole(inv_out),
                pl.BlockSpec((1, 1, root), lambda i: (i, 0, 0)),
            ]
            + [hbm] * len(after),
            out_specs=[fixed(n) for n in sizes],
            out_shape=[jax.ShapeDtypeStruct((count, n, cols, width), bf16) for n in sizes],
            scratch_shapes=[pltpu.VMEM((width // 128, root * cols, 128), f32)] * 2,
            compiler_params=params(),
            cost_estimate=cost(20),
            name="mixer_middle",
        )(*pieces, fwd_out, kernel_t, inv_out, twid_out, *after)

    def back(part, query, start, size, after):
        def local(i, pos):
            return jnp.where(i < size, 2 * i + 1 - pos[1], 2 * (i - size) + pos[1])

        def row(i, pos):
            return 2 * start + local(i, pos)

        shape = jax.ShapeDtypeStruct((size * root, width), bf16)
        return pl.pallas_call(
            functools.partial(mixer_back, size),
            grid_spec=pltpu.PrefetchScalarGridSpec(
                num_scalar_prefetch=1,
                grid=(2 * size,),
                in_specs=[pl.BlockSpec((count, 1, cols, width), lambda i, pos: (0, local(i, pos), 0, 0))]
                + [
                    whole(inv_in),
                    pl.BlockSpec((1, root, width), lambda i, pos: (0, row(i, pos), 0)),
                ]
                + [hbm] * len(after),
                out_specs=[
                    pl.BlockSpec((root, width), lambda i, pos: (jnp.minimum(i, size - 1), 0)),
                    pl.BlockSpec((root, width), lambda i, pos: (jnp.maximum(i - size, 0), 0)),
                ],
            ),
            out_shape=[shape] * 2,
            compiler_params=params(),
            cost_estimate=cost(1.8 * size),
            name="mixer_back",
        )(pos, part, inv_in, query, *after)

    out_shape = jax.ShapeDtypeStruct(stream.shape, bf16)

    def channels(s, start, size, own, got, x_got, out, after):
        flat = pl.BlockSpec((root, width), lambda i, pos: (i, 0))
        mine = pl.BlockSpec((1, root, width), lambda i, pos: (s, 2 * (start + i) + pos[1], 0))
        first = 0 if x_got.shape[0] == size * root else start
        theirs = pl.BlockSpec((root, width), lambda i, pos: (first + i, 0))
        args = [pos, own, got, stream, x_got, mix_tab, gain_out, up_tab, down_tab]
        specs = [flat, flat, mine, theirs, whole(mix_tab), whole(gain_out), whole(up_tab), whole(down_tab)]
        extra = list(after) + ([] if out is None else [out])
        args, specs = args + extra, specs + [hbm] * len(extra)
        return pl.pallas_call(
            mlp,
            grid_spec=pltpu.PrefetchScalarGridSpec(
                num_scalar_prefetch=1, grid=(size,), in_specs=specs, out_specs=[mine, flat]
            ),
            out_shape=[out_shape, jax.ShapeDtypeStruct((size * root, width), bf16)],
            input_output_aliases={} if out is None else {len(args) - 1: 0},
            compiler_params=params(),
            cost_estimate=cost(3.2 * size),
            name="mlp",
        )(*args)

    def placed(s, start, size, got, out):
        return pl.pallas_call(
            place,
            grid_spec=pltpu.PrefetchScalarGridSpec(
                num_scalar_prefetch=1,
                grid=(size,),
                in_specs=[pl.BlockSpec((root, width), lambda i, pos: (i, 0)), hbm],
                out_specs=pl.BlockSpec(
                    (1, root, width), lambda i, pos: (s, 2 * (start + i) + 1 - pos[1], 0)
                ),
            ),
            out_shape=out_shape,
            input_output_aliases={2: 0},
            compiler_params=params(),
            cost_estimate=cost(0.4 * size),
            name="place",
        )(pos, got, out)

    def cut(sizes):
        return [(sum(sizes[:i]), n) for i, n in enumerate(sizes)]

    into = [cut([rows // 4, rows - rows // 4])] + [cut([rows])] * (seqs - 1)
    outof = [cut([half])] * (seqs - 2) + [cut([half // 2, half // 2])] * 2

    firsts, queries, thirds, x_gots, gates, sent = {}, {}, {}, {}, {}, {}
    out = None
    last = None

    def swap_x(a):
        return lax.ppermute(a, "mp", swap)

    def upto(n):
        return line[n - 1 : n] if n else []

    def do_front(s, c=0, n=0, extra=()):
        nonlocal last
        start, size = into[s][c]
        rim, held = (rim_proj[s], ()) if c == 0 else queries[s]
        held, rim, part = front(
            s, start, size, rim, held, [*upto(n), *extra, *([] if last is None else [last])]
        )
        last = rim
        queries[s] = rim, held
        firsts[s, c] = part
        if c + 1 == len(into[s]):
            pieces = outof[s] if s == seqs - 1 else [(0, half)]
            x_gots[s] = [swap_x(held[1][a * root : (a + n) * root]) for a, n in pieces]

    def do_go(s, c=0, after=()):
        firsts[s, c] = exchanged(firsts[s, c], after)

    def do_middle(s, n=0, extra=()):
        nonlocal last
        pieces = [firsts[s, c] for c in range(len(into[s]))]
        res = middle(pieces, into[s], outof[s], [*upto(n), last, *extra])
        last = res[0]
        for c, part in enumerate(res):
            thirds[s, c] = part

    def do_send(s, c=0, after=()):
        thirds[s, c] = exchanged(thirds[s, c], after)

    def do_back(s, c=0, n=0, extra=()):
        nonlocal last
        start, size = outof[s][c]
        send, own = back(thirds[s, c], queries[s][1][0], start, size, [*upto(n), last, *extra])
        last = own
        gates[s, c] = own, swap_x(send)

    def do_mlp(s, c=0, n=0, extra=()):
        nonlocal last, out
        start, size = outof[s][c]
        out, send = channels(s, start, size, *gates[s, c], x_gots[s][c] if s == seqs - 1 else x_gots[s][0], out, [*upto(n), last, *extra])
        last = send
        sent[s, c] = swap_x(send)

    def do_place(s, c=0):
        nonlocal out
        out = placed(s, *outof[s][c], sent[s, c], out)

    do_front(0, 0)
    do_go(0, 0)
    do_front(0, 1, extra=[sums[1]])
    do_go(0, 1)
    do_front(1, n=1)
    do_go(1, 0, x_gots[0])
    do_middle(0, n=2)
    do_front(2, n=2)
    do_send(0, 0, [last, *x_gots[1], packed_got])
    do_middle(1, n=3)
    do_front(3, n=3)
    do_send(1, 0, [last, *x_gots[2], x_gots[3][0]])
    do_back(0, n=4)
    do_go(2, 0, [last, gates[0, 0][1]])
    do_back(1, n=5)
    do_mlp(0, n=5)
    do_go(3, 0, [last, gates[1, 0][1]])
    do_middle(2, n=6)
    do_mlp(1, n=6)
    do_send(2, 0, [last, sent[0, 0], x_gots[3][1]])
    do_middle(3, n=7)
    do_send(2, 1, [last, sent[1, 0]])
    do_back(2, 0, n=8)
    do_place(0)
    do_mlp(2, 0, n=8)
    do_send(3, 0, [last])
    do_back(2, 1, n=9)
    do_send(3, 1, [last, gates[2, 1][1], sent[2, 0]])
    do_back(3, 0, n=10)
    do_mlp(2, 1, n=10)
    do_back(3, 1)
    do_mlp(3, 0)
    do_mlp(3, 1, extra=[sent[2, 1]])
    do_place(1)
    do_place(2, 0)
    do_place(2, 1)
    do_place(3, 0)
    do_place(3, 1)
    return out


def from_behind(array, axis, by):
    length = lax.axis_size(axis)
    pairs = [(i, i + by) for i in range(length) if 0 <= i + by < length]
    return lax.ppermute(array, axis, pairs)


def plain_body(
    stream,
    gain_mix,
    proj_in,
    short_taps,
    fwd_inner,
    twid_inner,
    fwd_outer,
    kernel,
    inv_outer,
    backward_twiddle,
    inv_inner,
    proj_out,
    gain_mlp,
    up_blocks,
    down_blocks,
):
    seq_count, tok_count, width_here = stream.shape
    blocks_here, block_width = (proj_in.shape[0], proj_in.shape[1])
    root_len = fwd_inner.shape[0]
    rows_here = twid_inner.shape[0]
    sub_width = block_width // NB
    hid_block = up_blocks.shape[2]
    hid_sub = hid_block // NB
    x_float = stream.astype(jnp.float32)
    sumsq_mix = lax.psum(jnp.sum(x_float * x_float, axis=2), "mp")
    normed = (
        x_float * lax.rsqrt(sumsq_mix[..., None] / D + epsilon) * gain_mix.astype(jnp.float32)
    ).astype(jnp.bfloat16)
    u_blocks = normed.reshape(seq_count, tok_count, blocks_here, block_width)
    projected = jnp.einsum(
        "xtlc,lcd->xtld", u_blocks, proj_in, preferred_element_type=jnp.float32
    ).astype(jnp.bfloat16)
    rim_rows = projected[:, tok_count - 2 :]
    earlier = from_behind(rim_rows, "ctx", 1)
    padded = jnp.concatenate([earlier, projected], axis=1).astype(jnp.float32)
    mixed_all = (
        short_taps[0] * padded[:, 2:]
        + short_taps[1] * padded[:, 1 : tok_count + 1]
        + short_taps[2] * padded[:, :tok_count]
    )
    query_part = mixed_all[..., :block_width].astype(jnp.bfloat16)
    source = (
        mixed_all[..., block_width : 2 * block_width] * mixed_all[..., 2 * block_width :]
    ).astype(jnp.bfloat16)
    lattice = source.reshape(seq_count, rows_here, root_len, blocks_here, block_width)
    opening_segment = (
        jnp.einsum("xablc,bf->xaflc", lattice, fwd_inner, preferred_element_type=jnp.float32)
        * twid_inner[None, :, :, None, None]
    ).astype(jnp.bfloat16)
    kernel_blocks = kernel.reshape(root_len, kernel.shape[1], blocks_here, block_width)
    middle_segment = (
        jnp.einsum(
            "xaflc,ag->xgflc",
            lax.all_to_all(opening_segment, "ctx", split_axis=2, concat_axis=1, tiled=True),
            fwd_outer,
            preferred_element_type=jnp.float32,
        )
        * kernel_blocks[None]
    ).astype(jnp.bfloat16)
    closing_segment = (
        jnp.einsum("xgflc,gh->xhflc", middle_segment, inv_outer, preferred_element_type=jnp.float32)
        * backward_twiddle[None, :, :, None, None]
    ).astype(jnp.bfloat16)
    returned = lax.all_to_all(closing_segment, "ctx", split_axis=1, concat_axis=2, tiled=True)
    convolved = jnp.einsum(
        "xhflc,fe->lcxhe", returned, inv_inner, preferred_element_type=jnp.float32
    ).reshape(blocks_here, block_width, seq_count, tok_count)
    gated_out = (jnp.transpose(query_part, (2, 3, 0, 1)).astype(jnp.float32) * convolved).astype(
        jnp.bfloat16
    )
    spread = gated_out.reshape(blocks_here, NB, sub_width, seq_count, tok_count)
    out_table = proj_out.reshape(blocks_here, NB, sub_width, block_width)
    mix_out = jnp.einsum(
        "ijtxs,jitd->xsjd",
        lax.all_to_all(spread, "mp", split_axis=1, concat_axis=0, tiled=True),
        out_table,
        preferred_element_type=jnp.float32,
    )
    residual = (x_float.reshape(seq_count, tok_count, blocks_here, block_width) + mix_out).astype(
        jnp.bfloat16
    )
    resid_float = residual.astype(jnp.float32)
    sumsq_mlp = lax.psum(jnp.sum(resid_float * resid_float, axis=(2, 3)), "mp")
    gain_here = gain_mlp.astype(jnp.float32).reshape(blocks_here, block_width)
    normed_mlp = (
        resid_float * lax.rsqrt(sumsq_mlp[..., None, None] / D + epsilon) * gain_here
    ).astype(jnp.bfloat16)
    upper_part = jnp.einsum(
        "xslc,lch->lhxs", normed_mlp, up_blocks, preferred_element_type=jnp.float32
    )
    active = (
        jax.nn.gelu(upper_part)
        .astype(jnp.bfloat16)
        .reshape(blocks_here, NB, hid_sub, seq_count, tok_count)
    )
    down_table = down_blocks.reshape(blocks_here, NB, hid_sub, block_width)
    lower_part = jnp.einsum(
        "ijtxs,jitd->xsjd",
        lax.all_to_all(active, "mp", split_axis=1, concat_axis=0, tiled=True),
        down_table,
        preferred_element_type=jnp.float32,
    )
    output = (
        (resid_float + lower_part).astype(jnp.bfloat16).reshape(seq_count, tok_count, width_here)
    )
    return output


def solution(mesh):
    placed = (
        P(None, "ctx", "mp"),
        P("mp"),
        P("mp", None, None),
        P(None, "mp", None),
        P(),
        P("ctx", None),
        P(),
        P(None, "ctx", "mp"),
        P(),
        P(None, "ctx"),
        P(),
        P("mp", None, None),
        P("mp"),
        P("mp", None, None),
        P("mp", None, None),
    )
    sizes = dict(mesh.shape)
    tiled = ROOT // sizes["ctx"] % 16 == 0 and sizes["mp"] == 2
    return jax.shard_map(
        body if tiled else plain_body, mesh=mesh, in_specs=placed, out_specs=P(None, "ctx", "mp"), check_vma=False
    )
```
